256 devices in a mesh: ctx: 16 (over z, y_lo), exp: 16 (over y_hi, x, core).
Axes of the slice: x: 4, y: 4 (y_hi: 2, y_lo: 2; y = y_hi * 2 + y_lo), z: 8, core: 2. Of those that a mesh axis runs over, the one named last changes fastest.
Arguments:
- queries: bfloat16 [16, 2048, 4096], P('exp', 'ctx'), may hold values from -40 to 40
- keys_values: bfloat16 [16, 2048, 512], P('exp', 'ctx'), may hold values from -24 to 24
- norm_gain: float32 [4096], replicated, may hold values from 0.1 to 1.9
- routing: int32 [16, 2048, 8], P('exp', 'ctx'), may hold values from 0 to 127, all different within a row; in each aligned block of 128 rows (0 to 127, 128 to 255, ..., all dimensions but the last counted through in order) at most 9 rows name the same one
- gate_weights: float32 [16, 2048, 8], P('exp', 'ctx'), may hold values from 0.1 to 1
- expert_in: bfloat16 [256, 512, 2, 1536], P(('exp', 'ctx')), may hold values from -0.09375 to 0.09375
- expert_out: bfloat16 [256, 1536, 512], P(('exp', 'ctx')), may hold values from -0.15625 to 0.15625
Outputs:
- attended: bfloat16 [16, 2048, 4096], P('exp', 'ctx')
- expert_mix: bfloat16 [16, 2048, 4096], P('exp', 'ctx')
The draws below stay inside these ranges and needn't reach their ends.
Inputs may be any that keep to these rules, and one draw needn't show every extreme that they name: `routing`: each token names 8 different experts; the 128 tokens of one device name one expert at most 9 times.
All inputs are finite; a program needn't handle non-finite values.
Results may differ from the reference program's by a relative error of at most 0.03.
Values may be sent and summed in bfloat16 or wider, within the bound.
A program may use at most 128 MiB of HBM per device.

```python
import math
import jax
import jax.numpy as jnp
import numpy as np
from jax import lax

D = 4096
FF = 1536
HEAD = 128
TOP = 8
ROUTED = 128
QH = 32
KVH = 2
GROUP = 8
TOK_DEV = 128
SEQ = 2048
SEQS = 16
EXPERTS = 32
CAP = 9
N_CTX = 16
N_EXP = 16


def draw_queries(key, part):
    key = jax.random.fold_in(key, 1)
    values = jax.random.normal(key, (SEQS, SEQ, QH, HEAD), jnp.float32)
    values = jnp.clip(values, -40.0, 40.0)
    return values.reshape(SEQS, SEQ, QH * HEAD).astype(jnp.bfloat16)


def draw_keys_values(key, part):
    key = jax.random.fold_in(key, 2)
    keys = jax.random.normal(key, (SEQS, SEQ, KVH, HEAD), jnp.float32)
    vals = jax.random.normal(jax.random.fold_in(key, 3), (SEQS, SEQ, KVH * HEAD), jnp.float32)
    keys = jnp.clip(keys, -24.0, 24.0)
    vals = jnp.clip(vals, -24.0, 24.0)
    return jnp.concatenate([keys.reshape(SEQS, SEQ, KVH * HEAD), vals], axis=-1).astype(jnp.bfloat16)


def level_of(own_key, dims, cuts, smallest, high):
    gain = 1.0
    for position, blocks in cuts:
        draws = jax.random.uniform(jax.random.fold_in(jax.random.fold_in(own_key, 6), position), (blocks,), jnp.float32, smallest / len(cuts), high / len(cuts))
        gain = gain * jnp.repeat(jnp.exp(draws), dims[position] // blocks).reshape((-1,) + (1,) * (len(dims) - 1 - position))
    return gain


def routed_block(stream_key, own, number, rows, number_of, top, bound, skew):
    order = jax.random.permutation(stream_key, number_of)
    crowded, ordinary = load_shares(number_of, rows * top, bound, skew, True), load_shares(number_of, rows * top, bound, skew, False)
    places = jnp.arange(number_of)

    def named(sizes, offset_by):
        used = int((sizes > 0).sum())
        fixed = max(1, used // 4)
        shifted = fixed + (places - fixed + offset_by * (used - fixed)) % max(1, number_of - fixed)
        return jnp.zeros((number_of,), jnp.int32).at[order[jnp.where(places < fixed, places, shifted)]].set(jnp.asarray(sizes, jnp.int32))

    sizes = jnp.where(number % 4 == 0, named(crowded, number // 4), named(ordinary, number - number // 4 - 1))
    mixed = jax.random.permutation(jax.random.fold_in(own, 3), number_of)
    donor, taker = mixed[0:number_of // 2 * 2:2], mixed[1:number_of // 2 * 2:2]
    room = jnp.minimum(sizes[donor] - 1, bound - sizes[taker]) // 2
    room = jnp.where((donor == order[0]) | (taker == order[0]) | (sizes[taker] == 0), 0, jnp.maximum(room, 0))
    shifted = jax.random.randint(jax.random.fold_in(own, 4), (number_of // 2,), 0, 1 << 20) % (room + 1)
    sizes = sizes.at[donor].add(-shifted).at[taker].add(shifted)
    items = jnp.searchsorted(jnp.cumsum(sizes), jnp.arange(rows * top), side="right").astype(jnp.int32)
    table = items.reshape(top, rows).T
    table = table[jax.random.permutation(jax.random.fold_in(own, 1), rows)]
    offset_by = jax.random.randint(jax.random.fold_in(own, 2), (rows, 1), 0, top)
    return jnp.take_along_axis(table, (jnp.arange(top)[None, :] + offset_by) % top, axis=1)


def load_shares(amount, total, limit, skew, full):
    weights = [(1 << 20) // math.isqrt(rank ** skew) + 1 for rank in range(1, amount + 1)]
    largest = limit if full else min(limit, max(-(-total // amount), total * weights[0] // sum(weights)))
    least = 1 if total - largest >= amount - 1 else 0
    counts, spare = [largest] + [least] * (amount - 1), total - largest - least * (amount - 1)
    while spare > 0:
        free = [i for i in range(1, amount) if counts[i] < largest] or [i for i in range(1, amount) if counts[i] < limit]
        whole, left = sum([weights[i] for i in free]), spare
        for i in free:
            more = min(limit - counts[i], max(1, left * weights[i] // whole), spare)
            counts[i] = counts[i] + more
            spare = spare - more
    return np.array(counts)


def centred(own_key, shape, deviation, reach, cuts=(), kind=jnp.bfloat16):
    drawn = deviation * jax.random.normal(own_key, shape, jnp.float32)
    if cuts:
        drawn = drawn * level_of(own_key, shape, cuts, -0.22, 0.18)
    return jnp.clip(drawn, -reach, reach).astype(kind)


def setup_inputs(seed: int = 0) -> dict:
    key_list = jax.random.split(jax.random.key(seed), 8)
    queries = draw_queries(jax.random.fold_in(key_list[7], 71), 0)
    keys_values = draw_keys_values(jax.random.fold_in(key_list[7], 71), 0)
    norm_gain = jnp.clip(1.0 + 0.18 * jax.random.normal(key_list[2], (D,), jnp.float32), 0.1, 1.9)
    routing_keys = jax.random.split(jax.random.fold_in(key_list[3], 1), SEQS * SEQ // TOK_DEV)
    routing_turns = jax.random.permutation(jax.random.fold_in(key_list[3], 3), SEQS * SEQ // TOK_DEV)
    routing = jax.vmap(lambda own, number: routed_block(jax.random.fold_in(key_list[3], 2), own, number, TOK_DEV, ROUTED, TOP, CAP, 1))(routing_keys, routing_turns).reshape((SEQS, SEQ, TOP))
    gate_weights = jnp.clip(jnp.exp(math.log(1.0) - 2.3025851 * jax.random.uniform(key_list[4], (SEQS, SEQ, TOP), jnp.float32) ** level_of(key_list[4], (SEQS, SEQ, TOP), ((0, 16), (1, 16)), -0.2, 0.2)), 0.1, 1.0)
    expert_in = centred(key_list[5], (EXPERTS * GROUP, D // GROUP, 2, FF), D ** -0.5, 0.09375, ((0, 256),))
    expert_out = centred(key_list[6], (EXPERTS * GROUP, FF, D // GROUP), FF ** -0.5, 0.15625, ((0, 256),))
    return {"queries": queries, "keys_values": keys_values, "norm_gain": norm_gain, "routing": routing, "gate_weights": gate_weights, "expert_in": expert_in, "expert_out": expert_out}


def one_head(head_q, head_k, head_v):
    scores = jnp.dot(head_q, head_k.T, preferred_element_type=jnp.float32) / math.sqrt(HEAD)
    place = jnp.arange(SEQ, dtype=jnp.int32)
    allowed = place[None, :] <= place[:, None]
    scores = jnp.where(allowed, scores, -1e+30)
    highest = lax.optimization_barrier(jnp.max(scores, axis=1, keepdims=True))
    weights = jnp.where(allowed, jnp.exp(scores - highest), 0.0)
    total = lax.optimization_barrier(jnp.sum(weights, axis=1, keepdims=True))
    mixed = jnp.dot(weights.astype(jnp.bfloat16), head_v, preferred_element_type=jnp.float32)
    return mixed / total

def attend_sequence(pair):
    query_rows, kv_rows = pair
    heads = query_rows.reshape(SEQ, QH, HEAD).transpose(1, 0, 2)
    keys = kv_rows[:, :KVH * HEAD].reshape(SEQ, KVH, HEAD).transpose(1, 0, 2)
    vals = kv_rows[:, KVH * HEAD:].reshape(SEQ, KVH, HEAD).transpose(1, 0, 2)
    share = QH // KVH

    def per_head(index):
        group = index // share
        return one_head(heads[index], keys[group], vals[group])
    result = lax.map(per_head, jnp.arange(QH, dtype=jnp.int32))
    return result.transpose(1, 0, 2).reshape(SEQ, QH * HEAD).astype(jnp.bfloat16)

def reference(queries, keys_values, norm_gain, routing, gate_weights, expert_in, expert_out):
    attended = lax.map(attend_sequence, (queries, keys_values))
    values = attended.astype(jnp.float32)
    normed = (values * lax.rsqrt(lax.optimization_barrier(jnp.mean(values * values, axis=-1, keepdims=True)) + 1e-06) * norm_gain).astype(jnp.bfloat16)
    flat = normed.reshape(-1, D)
    routes = routing.reshape(-1)
    weights = gate_weights.reshape(-1)
    most = N_EXP * N_CTX * CAP
    width = D // GROUP
    levels = GROUP.bit_length() - 1

    def expert_step(carry, expert):
        hit = routes == expert
        chosen = jnp.nonzero(hit, size=most, fill_value=0)[0].astype(jnp.int32)
        live = jnp.arange(most, dtype=jnp.int32) < jnp.sum(hit.astype(jnp.int32))
        rows = flat[chosen // TOP]
        w_in = lax.dynamic_slice_in_dim(expert_in, (expert * GROUP).astype(jnp.int32), GROUP, 0)
        w_in = w_in.reshape(GROUP, width, 2 * FF)

        def one_slice(index):
            block = lax.dynamic_slice_in_dim(rows, (index * width).astype(jnp.int32), width, 1)
            return jnp.dot(block, w_in[index], preferred_element_type=jnp.float32).astype(jnp.bfloat16)
        current = lax.map(one_slice, jnp.arange(GROUP, dtype=jnp.int32))
        for level in range(levels):
            half = current.shape[0] // 2
            lower = lax.optimization_barrier(current[:half].astype(jnp.bfloat16)).astype(jnp.float32)
            upper = lax.optimization_barrier(current[half:].astype(jnp.bfloat16)).astype(jnp.float32)
            current = lower + upper
        gate_up = current[0].astype(jnp.float32)
        hidden = (jax.nn.silu(gate_up[:, :FF]) * gate_up[:, FF:]).astype(jnp.bfloat16)
        w_out = lax.dynamic_slice_in_dim(expert_out, (expert * GROUP).astype(jnp.int32), GROUP, 0)
        w_out = w_out.transpose(1, 0, 2).reshape(FF, D)
        produced = jnp.dot(hidden, w_out, preferred_element_type=jnp.float32).astype(jnp.bfloat16)
        factor = jnp.where(live, weights[chosen], 0.0)
        carry = carry.at[chosen // TOP].add(produced.astype(jnp.float32) * factor[:, None])
        return (carry, None)
    mixed, _ = lax.scan(expert_step, jnp.zeros((flat.shape[0], D), jnp.float32), jnp.arange(EXPERTS, dtype=jnp.int32))
    expert_mix = mixed.astype(jnp.bfloat16).reshape(SEQS, SEQ, D)
    return (attended, expert_mix)
```

```python
import functools
import math

import jax
import jax.numpy as jnp
from jax import lax
from jax.experimental import pallas as pl
from jax.experimental.pallas import tpu as pltpu
from jax.sharding import PartitionSpec as P

D = 4096
FF = 1536
HEAD = 128
TOP = 8
QH = 32
KVH = 2
GROUP = 8
CAP = 9
EXPERTS = 32
N_EXP = 16
N_Z = 8
ROWS = N_EXP * N_Z * CAP
HALF = ROWS // 2
CHUNK = 32
COUNT = HALF // CHUNK
PACK = 3
BLOCK = CHUNK * PACK
LAG = 2
TILE = 512
PART = D // 4
STRIPE = D // GROUP


def expert_kernel(x_ref, in_own, in_oth, out_own, out_oth, y_ref, part, recv, hid, s_send, s_recv, h_send, h_recv):
    c = lax.axis_index("ctx")
    side = c % 2
    place = (c // 2) % 4

    barrier = pltpu.get_barrier_semaphore()

    @pl.when(place > 0)
    def _():
        pl.semaphore_signal(barrier, inc=1, device_id={"ctx": c - 2}, device_id_type=pl.DeviceIdType.MESH)

    @pl.when(place < 3)
    def _():
        pl.semaphore_signal(barrier, inc=1, device_id={"ctx": c + 2}, device_id_type=pl.DeviceIdType.MESH)

    pl.semaphore_wait(barrier, jnp.where((place > 0) & (place < 3), 2, 1))

    own = pl.ds(pl.multiple_of(side * STRIPE, STRIPE), STRIPE)
    oth = pl.ds(pl.multiple_of((1 - side) * STRIPE, STRIPE), STRIPE)

    def sum_copy(d, i):
        target = jnp.where(d == 1, c + 2, c - 2)
        return pltpu.make_async_remote_copy(
            src_ref=part.at[d, i], dst_ref=recv.at[d, i], send_sem=s_send.at[d, i], recv_sem=s_recv.at[d, i],
            device_id={"ctx": target}, device_id_type=pl.DeviceIdType.MESH)

    def hid_copy(d, i):
        target = jnp.where(d == 1, c - 2, c + 2)
        return pltpu.make_async_remote_copy(
            src_ref=hid.at[d, i], dst_ref=hid.at[d, i], send_sem=h_send.at[d, i], recv_sem=h_recv.at[d, i],
            device_id={"ctx": target}, device_id_type=pl.DeviceIdType.MESH)

    def products(d, b):
        def tile(n, _):
            cols = pl.ds(pl.multiple_of(n * TILE, TILE), TILE)
            acc = jnp.dot(x_ref[d, b, :, own], in_own[:, cols], preferred_element_type=jnp.float32)
            acc += jnp.dot(x_ref[d, b, :, oth], in_oth[:, cols], preferred_element_type=jnp.float32)
            part[d, pl.ds(b * PACK, PACK), :, cols] = acc.astype(jnp.bfloat16).reshape(PACK, CHUNK, TILE)
            return 0
        lax.fori_loop(0, 2 * FF // TILE, tile, 0)

    def result(d, b):
        rows = hid[d, pl.ds(b * PACK, PACK)].reshape(BLOCK, FF)
        y_ref[d, b, :, own] = jnp.dot(rows, out_own[...], preferred_element_type=jnp.float32).astype(jnp.bfloat16)
        y_ref[d, b, :, oth] = jnp.dot(rows, out_oth[...], preferred_element_type=jnp.float32).astype(jnp.bfloat16)

    def step(t, _):
        @pl.when((t % PACK == 0) & (t < COUNT))
        def _():
            def both(d, _):
                products(d, t // PACK)
                return 0
            lax.fori_loop(0, 2, both, 0)

        def direction(d, _):
            pos = jnp.where(d == 1, place, 3 - place)
            i = t - LAG * pos

            @pl.when((i >= 0) & (i < COUNT))
            def _():
                @pl.when(pos == 0)
                def _():
                    sum_copy(d, i).start()

                @pl.when((pos > 0) & (pos < 3))
                def _():
                    sum_copy(d, i).wait_recv()
                    part[d, i] = (part[d, i].astype(jnp.float32) + recv[d, i].astype(jnp.float32)).astype(jnp.bfloat16)
                    sum_copy(d, i).start()

                @pl.when(pos == 3)
                def _():
                    sum_copy(d, i).wait_recv()
                    total = part[d, i].astype(jnp.float32) + recv[d, i].astype(jnp.float32)
                    gate = total[:, :FF]
                    hid[d, i] = (jax.nn.silu(gate) * total[:, FF:]).astype(jnp.bfloat16)
                    hid_copy(d, i).start()

            k = t - 3 * LAG - LAG * (3 - pos)

            @pl.when((k >= 0) & (k < COUNT))
            def _():
                @pl.when(pos < 3)
                def _():
                    hid_copy(d, k).wait_recv()

                @pl.when((pos > 0) & (pos < 3))
                def _():
                    hid_copy(d, k).start()

                @pl.when(k % PACK == PACK - 1)
                def _():
                    result(d, k // PACK)
            return 0

        lax.fori_loop(0, 2, direction, 0)
        return 0

    lax.fori_loop(0, COUNT + 6 * LAG, step, 0)

    def drain(i, _):
        def direction(d, _):
            pos = jnp.where(d == 1, place, 3 - place)

            @pl.when(pos < 3)
            def _():
                sum_copy(d, i).wait_send()

            @pl.when(pos > 0)
            def _():
                hid_copy(d, i).wait_send()
            return 0
        lax.fori_loop(0, 2, direction, 0)
        return 0

    lax.fori_loop(0, COUNT, drain, 0)


def experts(rows, in_own, in_oth, out_own, out_oth):
    vmem = pl.BlockSpec(memory_space=pltpu.VMEM)
    return pl.pallas_call(
        expert_kernel,
        out_shape=jax.ShapeDtypeStruct((2, COUNT // PACK, BLOCK, PART), jnp.bfloat16),
        in_specs=[vmem] * 5,
        out_specs=vmem,
        scratch_shapes=[
            pltpu.VMEM((2, COUNT, CHUNK, 2 * FF), jnp.bfloat16),
            pltpu.VMEM((2, COUNT, CHUNK, 2 * FF), jnp.bfloat16),
            pltpu.VMEM((2, COUNT, CHUNK, FF), jnp.bfloat16),
            pltpu.SemaphoreType.DMA((2, COUNT)),
            pltpu.SemaphoreType.DMA((2, COUNT)),
            pltpu.SemaphoreType.DMA((2, COUNT)),
            pltpu.SemaphoreType.DMA((2, COUNT)),
        ],
        compiler_params=pltpu.CompilerParams(collective_id=3, has_side_effects=True, vmem_limit_bytes=48 * 2**20),
        cost_estimate=pl.CostEstimate(flops=2 * ROWS * (PART * 2 * FF + FF * PART), bytes_accessed=14 * 2**20, transcendentals=HALF * FF),
        name="experts",
    )(rows.reshape(2, COUNT // PACK, BLOCK, PART), in_own, in_oth, out_own, out_oth).reshape(ROWS, PART)


def paired(array):
    return lax.ppermute(array, "ctx", [(i, i ^ 1) for i in range(16)])


def along_z(array):
    groups = [[2 * z + side for z in range(N_Z)] for side in range(2)]
    return lax.all_to_all(array, "ctx", split_axis=0, concat_axis=0, axis_index_groups=groups, tiled=True)


def along_exp(array):
    return lax.all_to_all(array, "exp", split_axis=0, concat_axis=0, tiled=True)


def attention(queries, keys_values):
    tok = queries.shape[1]
    share = QH // KVH
    first = lax.axis_index("ctx") * tok
    local_q = queries[0].reshape(tok, KVH, share, HEAD)
    query_place = first + jnp.arange(tok)

    def compute(state, block_rows, start):
        running, total, accum = state
        count = block_rows.shape[0]
        keys = block_rows[:, : KVH * HEAD].reshape(count, KVH, HEAD)
        vals = block_rows[:, KVH * HEAD :].reshape(count, KVH, HEAD)
        scores = jnp.einsum(
            "qkgh,nkh->kgqn", local_q, keys, preferred_element_type=jnp.float32
        ) / math.sqrt(HEAD)
        allowed = (start + jnp.arange(count))[None, :] <= query_place[:, None]
        scores = jnp.where(allowed, scores, -1e30)
        newest = jnp.maximum(running, jnp.max(scores, axis=-1))
        keep = jnp.exp(running - newest)
        weights = jnp.where(allowed, jnp.exp(scores - newest[..., None]), 0.0)
        total = total * keep + jnp.sum(weights, axis=-1)
        accum = accum * keep[..., None] + jnp.einsum(
            "kgqn,nkh->kgqh", weights.astype(jnp.bfloat16), vals, preferred_element_type=jnp.float32
        )
        return (newest, total, accum)

    initial = (
        jnp.full((KVH, share, tok), -1e30, jnp.float32),
        jnp.zeros((KVH, share, tok), jnp.float32),
        jnp.zeros((KVH, share, tok, HEAD), jnp.float32),
    )
    piece = lax.all_gather(keys_values, "ctx", axis=1, tiled=True)
    count = piece.shape[1]
    block = tok * 4
    blocks = piece[0].reshape(count // block, block, piece.shape[2])

    def visit(index, kept):
        block_rows = lax.dynamic_index_in_dim(blocks, index, 0, keepdims=False)
        block_start = index * block
        return lax.cond(
            block_start > first + tok - 1,
            lambda inner: inner,
            lambda inner: compute(inner, block_rows, block_start),
            kept,
        )

    running, total, accum = lax.fori_loop(0, count // block, visit, initial)
    return (
        (accum / total[..., None])
        .transpose(2, 0, 1, 3)
        .reshape(tok, QH * HEAD)
        .astype(jnp.bfloat16)
    )


def local(queries, keys_values, norm_gain, routing, gate_weights, expert_in, expert_out):
    tok = queries.shape[1]
    in_own = expert_in[0].reshape(STRIPE, 2 * FF)
    out_own = expert_out[0]
    in_oth = paired(in_own)
    out_oth = paired(out_own)

    same = routing[0][:, :, None] == jnp.arange(EXPERTS)[None, None, :]
    gates = jnp.sum(jnp.where(same, gate_weights[0][:, :, None], 0.0), axis=1)
    hit = jnp.any(same, axis=1)
    earlier = jnp.arange(tok)[:, None] > jnp.arange(tok)[None, :]
    slot = jnp.dot(earlier.astype(jnp.bfloat16), hit.astype(jnp.bfloat16), preferred_element_type=jnp.float32)
    chosen = hit[:, :, None] & (slot[:, :, None] == jnp.arange(CAP, dtype=jnp.float32)[None, None, :])
    chosen = chosen.reshape(tok, N_EXP, 2, CAP).transpose(0, 2, 1, 3)
    spread = jnp.where(chosen, gates.reshape(tok, N_EXP, 2, 1).transpose(0, 2, 1, 3), 0.0).reshape(tok, EXPERTS * CAP)
    pick = chosen.reshape(tok, EXPERTS * CAP).astype(jnp.bfloat16)
    high = lax.reduce_precision(spread, 8, 7)
    low = spread - high
    spread = jnp.concatenate([high, low], axis=0).astype(jnp.bfloat16)

    attended = attention(queries, keys_values)
    values = attended.astype(jnp.float32)
    normed = (
        values * lax.rsqrt(jnp.mean(values * values, axis=-1, keepdims=True) + 1e-06) * norm_gain
    ).astype(jnp.bfloat16)

    outgoing = lax.dot_general(pick, normed, (((0,), (0,)), ((), ())), preferred_element_type=jnp.float32)
    outgoing = outgoing.astype(jnp.bfloat16).reshape(2, N_EXP * CAP, 4, PART).transpose(0, 2, 1, 3)
    middle = along_z(outgoing.reshape(N_Z, N_EXP * CAP, PART))
    middle = middle.reshape(N_Z, N_EXP, CAP, PART).transpose(1, 0, 2, 3)
    rows = along_exp(middle.reshape(N_EXP, N_Z * CAP, PART)).reshape(ROWS, PART)

    made = experts(rows, in_own, in_oth, out_own, out_oth)

    middle = along_exp(made.reshape(N_EXP, N_Z * CAP, PART))
    middle = middle.reshape(N_EXP, N_Z, CAP, PART).transpose(1, 0, 2, 3)
    back = along_z(middle.reshape(N_Z, N_EXP * CAP, PART))
    back = back.reshape(2, 4, N_EXP * CAP, PART).transpose(0, 2, 1, 3).reshape(EXPERTS * CAP, D)
    mixed = jnp.dot(spread, back, preferred_element_type=jnp.float32)
    mixed = mixed[:tok] + mixed[tok:]
    return (attended[None], mixed.astype(jnp.bfloat16)[None])


def solution(mesh):
    in_specs = (
        P("exp", "ctx", None),
        P("exp", "ctx", None),
        P(),
        P("exp", "ctx", None),
        P("exp", "ctx", None),
        P(("exp", "ctx"), None, None, None),
        P(("exp", "ctx"), None, None),
    )
    out_specs = (P("exp", "ctx", None), P("exp", "ctx", None))
    return jax.shard_map(local, mesh=mesh, in_specs=in_specs, out_specs=out_specs, check_vma=False)
```

```python
import functools
import math

import jax
import jax.numpy as jnp
from jax import lax
from jax.experimental import pallas as pl
from jax.experimental.pallas import tpu as pltpu
from jax.sharding import PartitionSpec as P

D = 4096
FF = 1536
HEAD = 128
TOP = 8
QH = 32
KVH = 2
GROUP = 8
CAP = 9
EXPERTS = 32
N_EXP = 16
N_Z = 8
ROWS = N_EXP * N_Z * CAP
HALF = ROWS // 2
CHUNK = 32
COUNT = HALF // CHUNK
PACK = 3
BLOCK = CHUNK * PACK
LAG = 2
TILE = 512
PART = D // 4
STRIPE = D // GROUP


def expert_kernel(x_ref, in_own, in_one, in_two, out_own, y_ref, part, recv, hid, out_oth, s_send, s_recv, h_send, h_recv, w_sems):
    c = lax.axis_index("ctx")
    side = c % 2
    place = (c // 2) % 4

    barrier = pltpu.get_barrier_semaphore()

    @pl.when(place > 0)
    def _():
        pl.semaphore_signal(barrier, inc=1, device_id={"ctx": c - 2}, device_id_type=pl.DeviceIdType.MESH)

    @pl.when(place < 3)
    def _():
        pl.semaphore_signal(barrier, inc=1, device_id={"ctx": c + 2}, device_id_type=pl.DeviceIdType.MESH)

    pl.semaphore_signal(barrier, inc=1, device_id={"ctx": c + 1 - 2 * side}, device_id_type=pl.DeviceIdType.MESH)
    pl.semaphore_wait(barrier, jnp.where((place > 0) & (place < 3), 3, 2))
    weights = pltpu.make_async_remote_copy(
        src_ref=out_own, dst_ref=out_oth, send_sem=w_sems.at[0], recv_sem=w_sems.at[1],
        device_id={"ctx": c + 1 - 2 * side}, device_id_type=pl.DeviceIdType.MESH)
    weights.start()

    own = pl.ds(pl.multiple_of(side * STRIPE, STRIPE), STRIPE)
    oth = pl.ds(pl.multiple_of((1 - side) * STRIPE, STRIPE), STRIPE)
    one = pl.ds(pl.multiple_of((1 - side) * STRIPE, STRIPE), STRIPE // 2)
    two = pl.ds(pl.multiple_of((1 - side) * STRIPE + STRIPE // 2, STRIPE // 2), STRIPE // 2)

    def sum_copy(d, i):
        target = jnp.where(d == 1, c + 2, c - 2)
        return pltpu.make_async_remote_copy(
            src_ref=part.at[d, i], dst_ref=recv.at[d, i], send_sem=s_send.at[d, i], recv_sem=s_recv.at[d, i],
            device_id={"ctx": target}, device_id_type=pl.DeviceIdType.MESH)

    def hid_copy(d, i):
        target = jnp.where(d == 1, c - 2, c + 2)
        return pltpu.make_async_remote_copy(
            src_ref=hid.at[d, i], dst_ref=hid.at[d, i], send_sem=h_send.at[d, i], recv_sem=h_recv.at[d, i],
            device_id={"ctx": target}, device_id_type=pl.DeviceIdType.MESH)

    def products(d, b):
        def tile(n, _):
            cols = pl.ds(pl.multiple_of(n * TILE, TILE), TILE)
            acc = jnp.dot(x_ref[d, b, :, own], in_own[:, cols], preferred_element_type=jnp.float32)
            acc += jnp.dot(x_ref[d, b, :, one], in_one[:, cols], preferred_element_type=jnp.float32)
            acc += jnp.dot(x_ref[d, b, :, two], in_two[:, cols], preferred_element_type=jnp.float32)
            part[d, pl.ds(b * PACK, PACK), :, cols] = acc.astype(jnp.bfloat16).reshape(PACK, CHUNK, TILE)
            return 0
        lax.fori_loop(0, 2 * FF // TILE, tile, 0)

    def result(d, b):
        rows = hid[d, pl.ds(b * PACK, PACK)].reshape(BLOCK, FF)
        y_ref[d, b, :, own] = jnp.dot(rows, out_own[...], preferred_element_type=jnp.float32).astype(jnp.bfloat16)
        y_ref[d, b, :, oth] = jnp.dot(rows, out_oth[...], preferred_element_type=jnp.float32).astype(jnp.bfloat16)

    def step(t, _):
        @pl.when((t % PACK == 0) & (t < COUNT))
        def _():
            def both(d, _):
                products(d, t // PACK)
                return 0
            lax.fori_loop(0, 2, both, 0)

        @pl.when(t == 3 * LAG + PACK - 1)
        def _():
            weights.wait_recv()

        def direction(d, _):
            pos = jnp.where(d == 1, place, 3 - place)
            i = t - LAG * pos

            @pl.when((i >= 0) & (i < COUNT))
            def _():
                @pl.when(pos == 0)
                def _():
                    sum_copy(d, i).start()

                @pl.when((pos > 0) & (pos < 3))
                def _():
                    sum_copy(d, i).wait_recv()
                    part[d, i] = (part[d, i].astype(jnp.float32) + recv[d, i].astype(jnp.float32)).astype(jnp.bfloat16)
                    sum_copy(d, i).start()

                @pl.when(pos == 3)
                def _():
                    sum_copy(d, i).wait_recv()
                    total = part[d, i].astype(jnp.float32) + recv[d, i].astype(jnp.float32)
                    gate = total[:, :FF]
                    hid[d, i] = (jax.nn.silu(gate) * total[:, FF:]).astype(jnp.bfloat16)
                    hid_copy(d, i).start()

            k = t - 3 * LAG - LAG * (3 - pos)

            @pl.when((k >= 0) & (k < COUNT))
            def _():
                @pl.when(pos < 3)
                def _():
                    hid_copy(d, k).wait_recv()

                @pl.when((pos > 0) & (pos < 3))
                def _():
                    hid_copy(d, k).start()

                @pl.when(k % PACK == PACK - 1)
                def _():
                    result(d, k // PACK)
            return 0

        lax.fori_loop(0, 2, direction, 0)
        return 0

    lax.fori_loop(0, COUNT + 6 * LAG, step, 0)

    def drain(i, _):
        def direction(d, _):
            pos = jnp.where(d == 1, place, 3 - place)

            @pl.when(pos < 3)
            def _():
                sum_copy(d, i).wait_send()

            @pl.when(pos > 0)
            def _():
                hid_copy(d, i).wait_send()
            return 0
        lax.fori_loop(0, 2, direction, 0)
        return 0

    lax.fori_loop(0, COUNT, drain, 0)
    weights.wait_send()


def experts(rows, in_own, in_one, in_two, out_own):
    vmem = pl.BlockSpec(memory_space=pltpu.VMEM)
    return pl.pallas_call(
        expert_kernel,
        out_shape=jax.ShapeDtypeStruct((2, COUNT // PACK, BLOCK, PART), jnp.bfloat16),
        in_specs=[vmem] * 5,
        out_specs=vmem,
        scratch_shapes=[
            pltpu.VMEM((2, COUNT, CHUNK, 2 * FF), jnp.bfloat16),
            pltpu.VMEM((2, COUNT, CHUNK, 2 * FF), jnp.bfloat16),
            pltpu.VMEM((2, COUNT, CHUNK, FF), jnp.bfloat16),
            pltpu.VMEM((FF, STRIPE), jnp.bfloat16),
            pltpu.SemaphoreType.DMA((2, COUNT)),
            pltpu.SemaphoreType.DMA((2, COUNT)),
            pltpu.SemaphoreType.DMA((2, COUNT)),
            pltpu.SemaphoreType.DMA((2, COUNT)),
            pltpu.SemaphoreType.DMA((2,)),
        ],
        compiler_params=pltpu.CompilerParams(collective_id=3, has_side_effects=True, vmem_limit_bytes=48 * 2**20),
        cost_estimate=pl.CostEstimate(flops=2 * ROWS * (PART * 2 * FF + FF * PART), bytes_accessed=14 * 2**20, transcendentals=HALF * FF),
        name="experts",
    )(rows.reshape(2, COUNT // PACK, BLOCK, PART), in_own, in_one, in_two, out_own).reshape(ROWS, PART)


def exchange_kernel(*refs):
    if len(refs) == 7:
        give_ref, half_ref, take_ref, got_ref, sends, recvs, keep = refs
    else:
        give_ref, take_ref, sends, recvs, keep = refs
    c = lax.axis_index("ctx")
    e = lax.axis_index("exp")
    side, z = c % 2, c // 2
    core, x, y = e % 2, (e // 2) % 4, e // 8
    me = e * N_Z + z
    total = N_EXP * N_Z

    def partner(o):
        s, g = o % N_Z, o // N_Z
        dz = jnp.where(s % 2 == 1, (s + 1) // 2, (N_Z - s // 2) % N_Z)
        there = (y + g // 8) % 2 * 8 + (x + (g // 2) % 4) % 4 * 2 + (core + g % 2) % 2
        return there, (z + dz) % N_Z

    def other_half():
        return pltpu.make_async_remote_copy(
            src_ref=half_ref, dst_ref=got_ref, send_sem=sends.at[1], recv_sem=recvs.at[1],
            device_id={"ctx": c + 1 - 2 * side}, device_id_type=pl.DeviceIdType.MESH)

    barrier = pltpu.get_barrier_semaphore()

    def greet(o, _):
        pe, pz = partner(o)
        pl.semaphore_signal(barrier, inc=1, device_id={"exp": pe, "ctx": 2 * pz + side}, device_id_type=pl.DeviceIdType.MESH)
        return 0

    lax.fori_loop(1, total, greet, 0)
    if len(refs) == 7:
        pl.semaphore_signal(barrier, inc=1, device_id={"ctx": c + 1 - 2 * side}, device_id_type=pl.DeviceIdType.MESH)
        pl.semaphore_wait(barrier, total)
        other_half().start()
    else:
        pl.semaphore_wait(barrier, total - 1)

    def send(o, _):
        pe, pz = partner(o)
        pltpu.make_async_remote_copy(
            src_ref=give_ref.at[pe * N_Z + pz], dst_ref=take_ref.at[me], send_sem=sends.at[0], recv_sem=recvs.at[0],
            device_id={"exp": pe, "ctx": 2 * pz + side}, device_id_type=pl.DeviceIdType.MESH).start()
        return 0

    lax.fori_loop(1, total, send, 0)
    stay = pltpu.make_async_copy(give_ref.at[me], take_ref.at[me], keep)
    stay.start()
    stay.wait()
    rest = pltpu.make_async_remote_copy(
        src_ref=give_ref.at[pl.ds(0, total - 1)], dst_ref=take_ref.at[pl.ds(0, total - 1)], send_sem=sends.at[0],
        recv_sem=recvs.at[0], device_id={"ctx": c + 1 - 2 * side}, device_id_type=pl.DeviceIdType.MESH)
    rest.wait_recv()
    rest.wait_send()
    if len(refs) == 7:
        other_half().wait()


def exchanged(blocks, half=None):
    vmem = pl.BlockSpec(memory_space=pltpu.VMEM)
    given = [blocks] if half is None else [blocks, half]
    shapes = [jax.ShapeDtypeStruct(g.shape, g.dtype) for g in given]
    got = pl.pallas_call(
        exchange_kernel,
        out_shape=shapes,
        in_specs=[vmem] * len(given),
        out_specs=[vmem] * len(given),
        scratch_shapes=[pltpu.SemaphoreType.DMA((2,)), pltpu.SemaphoreType.DMA((2,)), pltpu.SemaphoreType.DMA],
        compiler_params=pltpu.CompilerParams(collective_id=4 + len(given), has_side_effects=True, vmem_limit_bytes=24 * 2**20),
        cost_estimate=pl.CostEstimate(flops=0, bytes_accessed=16 * 2**20, transcendentals=0),
        name="dispatch" if half is not None else "giveback",
    )(*given)
    return got


def attention(queries, keys_values):
    tok = queries.shape[1]
    share = QH // KVH
    first = lax.axis_index("ctx") * tok
    local_q = queries[0].reshape(tok, KVH, share, HEAD)
    query_place = first + jnp.arange(tok)

    def compute(state, block_rows, start):
        running, total, accum = state
        count = block_rows.shape[0]
        keys = block_rows[:, : KVH * HEAD].reshape(count, KVH, HEAD)
        vals = block_rows[:, KVH * HEAD :].reshape(count, KVH, HEAD)
        scores = jnp.einsum(
            "qkgh,nkh->kgqn", local_q, keys, preferred_element_type=jnp.float32
        ) / math.sqrt(HEAD)
        allowed = (start + jnp.arange(count))[None, :] <= query_place[:, None]
        scores = jnp.where(allowed, scores, -1e30)
        newest = jnp.maximum(running, jnp.max(scores, axis=-1))
        keep = jnp.exp(running - newest)
        weights = jnp.where(allowed, jnp.exp(scores - newest[..., None]), 0.0)
        total = total * keep + jnp.sum(weights, axis=-1)
        accum = accum * keep[..., None] + jnp.einsum(
            "kgqn,nkh->kgqh", weights.astype(jnp.bfloat16), vals, preferred_element_type=jnp.float32
        )
        return (newest, total, accum)

    initial = (
        jnp.full((KVH, share, tok), -1e30, jnp.float32),
        jnp.zeros((KVH, share, tok), jnp.float32),
        jnp.zeros((KVH, share, tok, HEAD), jnp.float32),
    )
    piece = lax.all_gather(keys_values, "ctx", axis=1, tiled=True)
    count = piece.shape[1]
    block = tok * 4
    blocks = piece[0].reshape(count // block, block, piece.shape[2])

    def visit(index, kept):
        block_rows = lax.dynamic_index_in_dim(blocks, index, 0, keepdims=False)
        block_start = index * block
        return lax.cond(
            block_start > first + tok - 1,
            lambda inner: inner,
            lambda inner: compute(inner, block_rows, block_start),
            kept,
        )

    running, total, accum = lax.fori_loop(0, count // block, visit, initial)
    return (
        (accum / total[..., None])
        .transpose(2, 0, 1, 3)
        .reshape(tok, QH * HEAD)
        .astype(jnp.bfloat16)
    )


def local(queries, keys_values, norm_gain, routing, gate_weights, expert_in, expert_out):
    tok = queries.shape[1]
    in_own = expert_in[0].reshape(STRIPE, 2 * FF)
    out_own = expert_out[0]
    in_one = lax.ppermute(in_own[: STRIPE // 2], "ctx", [(i, i ^ 1) for i in range(16)])

    same = routing[0][:, :, None] == jnp.arange(EXPERTS)[None, None, :]
    gates = jnp.sum(jnp.where(same, gate_weights[0][:, :, None], 0.0), axis=1)
    hit = jnp.any(same, axis=1)
    earlier = jnp.arange(tok)[:, None] > jnp.arange(tok)[None, :]
    slot = jnp.dot(earlier.astype(jnp.bfloat16), hit.astype(jnp.bfloat16), preferred_element_type=jnp.float32)
    chosen = hit[:, :, None] & (slot[:, :, None] == jnp.arange(CAP, dtype=jnp.float32)[None, None, :])
    spread = jnp.where(chosen, gates[:, :, None], 0.0).reshape(tok, EXPERTS * CAP)
    pick = chosen.reshape(tok, EXPERTS * CAP).astype(jnp.bfloat16)
    high = lax.reduce_precision(spread, 8, 7)
    low = spread - high
    spread = jnp.concatenate([high, low], axis=0).astype(jnp.bfloat16)

    attended = attention(queries, keys_values)
    values = attended.astype(jnp.float32)
    normed = (
        values * lax.rsqrt(jnp.mean(values * values, axis=-1, keepdims=True) + 1e-06) * norm_gain
    ).astype(jnp.bfloat16)

    outgoing = lax.dot_general(pick, normed, (((0,), (0,)), ((), ())), preferred_element_type=jnp.float32)
    outgoing = outgoing.astype(jnp.bfloat16).reshape(N_EXP, 2, CAP, 4, 8, 128).transpose(0, 1, 3, 2, 4, 5)
    rows, in_two = exchanged(outgoing.reshape(N_EXP * N_Z, CAP, 8, 128), in_own[STRIPE // 2 :])

    made = experts(rows.reshape(ROWS, PART), in_own, in_one, in_two, out_own)

    (back,) = exchanged(made.reshape(N_EXP * N_Z, CAP, 8, 128))
    back = back.reshape(N_EXP, 2, 4, CAP, 8, 128).transpose(0, 1, 3, 2, 4, 5).reshape(EXPERTS * CAP, D)
    mixed = jnp.dot(spread, back, preferred_element_type=jnp.float32)
    mixed = mixed[:tok] + mixed[tok:]
    return (attended[None], mixed.astype(jnp.bfloat16)[None])


def solution(mesh):
    in_specs = (
        P("exp", "ctx", None),
        P("exp", "ctx", None),
        P(),
        P("exp", "ctx", None),
        P("exp", "ctx", None),
        P(("exp", "ctx"), None, None, None),
        P(("exp", "ctx"), None, None),
    )
    out_specs = (P("exp", "ctx", None), P("exp", "ctx", None))
    return jax.shard_map(local, mesh=mesh, in_specs=in_specs, out_specs=out_specs, check_vma=False)
```

```python
import functools
import math

import jax
import jax.numpy as jnp
from jax import lax
from jax.experimental import pallas as pl
from jax.experimental.pallas import tpu as pltpu
from jax.sharding import PartitionSpec as P

D = 4096
FF = 1536
HEAD = 128
TOP = 8
QH = 32
KVH = 2
GROUP = 8
CAP = 9
EXPERTS = 32
TOK = 128
SLOTS = EXPERTS * CAP
N_EXP = 16
N_Z = 8
ROWS = N_EXP * N_Z * CAP
HALF = ROWS // 2
CHUNK = 16
COUNT = HALF // CHUNK
PACK = 9
BLOCK = CHUNK * PACK
LAG = 2
TILE = 512
PART = D // 4
STRIPE = D // GROUP
GATHER = BLOCK // CAP


def expert_kernel(x_ref, in_own, in_one, in_two, out_own, y_ref, part, recv, hid, out_oth, flat, xb, s_send, s_recv, h_send, h_recv, w_sems):
    c = lax.axis_index("ctx")
    side = c % 2
    place = (c // 2) % 4

    barrier = pltpu.get_barrier_semaphore()

    @pl.when(place > 0)
    def _():
        pl.semaphore_signal(barrier, inc=1, device_id={"ctx": c - 2}, device_id_type=pl.DeviceIdType.MESH)

    @pl.when(place < 3)
    def _():
        pl.semaphore_signal(barrier, inc=1, device_id={"ctx": c + 2}, device_id_type=pl.DeviceIdType.MESH)

    pl.semaphore_signal(barrier, inc=1, device_id={"ctx": c + 1 - 2 * side}, device_id_type=pl.DeviceIdType.MESH)
    pl.semaphore_wait(barrier, jnp.where((place > 0) & (place < 3), 3, 2))
    weights = pltpu.make_async_remote_copy(
        src_ref=out_own, dst_ref=out_oth, send_sem=w_sems.at[0], recv_sem=w_sems.at[1],
        device_id={"ctx": c + 1 - 2 * side}, device_id_type=pl.DeviceIdType.MESH)
    weights.start()

    own = pl.ds(pl.multiple_of(side * STRIPE, STRIPE), STRIPE)
    oth = pl.ds(pl.multiple_of((1 - side) * STRIPE, STRIPE), STRIPE)
    one = pl.ds(pl.multiple_of((1 - side) * STRIPE, STRIPE), STRIPE // 2)
    two = pl.ds(pl.multiple_of((1 - side) * STRIPE + STRIPE // 2, STRIPE // 2), STRIPE // 2)

    def sum_copy(d, i):
        target = jnp.where(d == 1, c + 2, c - 2)
        return pltpu.make_async_remote_copy(
            src_ref=part.at[d, i], dst_ref=recv.at[d, i], send_sem=s_send.at[d, i], recv_sem=s_recv.at[d, i],
            device_id={"ctx": target}, device_id_type=pl.DeviceIdType.MESH)

    def hid_copy(d, i):
        target = jnp.where(d == 1, c - 2, c + 2)
        return pltpu.make_async_remote_copy(
            src_ref=hid.at[d, i], dst_ref=hid.at[d, i], send_sem=h_send.at[d, i], recv_sem=h_recv.at[d, i],
            device_id={"ctx": target}, device_id_type=pl.DeviceIdType.MESH)

    def products(d, b):
        flat[...] = x_ref[d, b].astype(jnp.float32).reshape(8 * BLOCK, 128)
        for k in range(8):
            xb[:, k * 128 : (k + 1) * 128] = flat[pl.ds(k, BLOCK, stride=8), :].astype(jnp.bfloat16)

        def tile(n, _):
            cols = pl.ds(pl.multiple_of(n * TILE, TILE), TILE)
            acc = jnp.dot(xb[:, own], in_own[:, cols], preferred_element_type=jnp.float32)
            acc += jnp.dot(xb[:, one], in_one[:, cols], preferred_element_type=jnp.float32)
            acc += jnp.dot(xb[:, two], in_two[:, cols], preferred_element_type=jnp.float32)
            part[d, pl.ds(b * PACK, PACK), :, cols] = acc.astype(jnp.bfloat16).reshape(PACK, CHUNK, TILE)
            return 0
        lax.fori_loop(0, 2 * FF // TILE, tile, 0)

    def result(d, b):
        rows = hid[d, pl.ds(b * PACK, PACK)].reshape(BLOCK, FF)
        mine = jnp.dot(rows, out_own[...], preferred_element_type=jnp.float32)
        theirs = jnp.dot(rows, out_oth[...], preferred_element_type=jnp.float32)
        for k in range(4):
            cols = slice(k * 128, (k + 1) * 128)
            flat[pl.ds(k, BLOCK, stride=8), :] = jnp.where(side == 0, mine[:, cols], theirs[:, cols])
            flat[pl.ds(k + 4, BLOCK, stride=8), :] = jnp.where(side == 0, theirs[:, cols], mine[:, cols])
        y_ref[d, b] = flat[...].astype(jnp.bfloat16).reshape(GATHER, CAP, 8, 128)

    def step(t, _):
        @pl.when((t % PACK == 0) & (t < COUNT))
        def _():
            def both(d, _):
                products(d, t // PACK)
                return 0
            lax.fori_loop(0, 2, both, 0)

        @pl.when(t == 3 * LAG + PACK - 1)
        def _():
            weights.wait_recv()

        def direction(d, _):
            pos = jnp.where(d == 1, place, 3 - place)
            i = t - LAG * pos

            @pl.when((i >= 0) & (i < COUNT))
            def _():
                @pl.when(pos == 0)
                def _():
                    sum_copy(d, i).start()

                @pl.when((pos > 0) & (pos < 3))
                def _():
                    sum_copy(d, i).wait_recv()
                    part[d, i] = (part[d, i].astype(jnp.float32) + recv[d, i].astype(jnp.float32)).astype(jnp.bfloat16)
                    sum_copy(d, i).start()

                @pl.when(pos == 3)
                def _():
                    sum_copy(d, i).wait_recv()
                    total = part[d, i].astype(jnp.float32) + recv[d, i].astype(jnp.float32)
                    gate = total[:, :FF]
                    hid[d, i] = (jax.nn.silu(gate) * total[:, FF:]).astype(jnp.bfloat16)
                    hid_copy(d, i).start()

            k = t - 3 * LAG - LAG * (3 - pos)

            @pl.when((k >= 0) & (k < COUNT))
            def _():
                @pl.when(pos < 3)
                def _():
                    hid_copy(d, k).wait_recv()

                @pl.when((pos > 0) & (pos < 3))
                def _():
                    hid_copy(d, k).start()

                @pl.when(k % PACK == PACK - 1)
                def _():
                    result(d, k // PACK)
            return 0

        lax.fori_loop(0, 2, direction, 0)
        return 0

    lax.fori_loop(0, COUNT + 6 * LAG, step, 0)

    def drain(i, _):
        def direction(d, _):
            pos = jnp.where(d == 1, place, 3 - place)

            @pl.when(pos < 3)
            def _():
                sum_copy(d, i).wait_send()

            @pl.when(pos > 0)
            def _():
                hid_copy(d, i).wait_send()
            return 0
        lax.fori_loop(0, 2, direction, 0)
        return 0

    lax.fori_loop(0, COUNT, drain, 0)
    weights.wait_send()


def experts(rows, in_own, in_one, in_two, out_own):
    vmem = pl.BlockSpec(memory_space=pltpu.VMEM)
    return pl.pallas_call(
        expert_kernel,
        out_shape=jax.ShapeDtypeStruct((2, COUNT // PACK, GATHER, CAP, 8, 128), jnp.bfloat16),
        in_specs=[vmem] * 5,
        out_specs=vmem,
        scratch_shapes=[
            pltpu.VMEM((2, COUNT, CHUNK, 2 * FF), jnp.bfloat16),
            pltpu.VMEM((2, COUNT, CHUNK, 2 * FF), jnp.bfloat16),
            pltpu.VMEM((2, COUNT, CHUNK, FF), jnp.bfloat16),
            pltpu.VMEM((FF, STRIPE), jnp.bfloat16),
            pltpu.VMEM((8 * BLOCK, 128), jnp.float32),
            pltpu.VMEM((BLOCK, PART), jnp.bfloat16),
            pltpu.SemaphoreType.DMA((2, COUNT)),
            pltpu.SemaphoreType.DMA((2, COUNT)),
            pltpu.SemaphoreType.DMA((2, COUNT)),
            pltpu.SemaphoreType.DMA((2, COUNT)),
            pltpu.SemaphoreType.DMA((2,)),
        ],
        compiler_params=pltpu.CompilerParams(collective_id=3, has_side_effects=True, vmem_limit_bytes=48 * 2**20),
        cost_estimate=pl.CostEstimate(flops=2 * ROWS * (PART * 2 * FF + FF * PART), bytes_accessed=14 * 2**20, transcendentals=HALF * FF),
        name="experts",
    )(rows.reshape(2, COUNT // PACK, GATHER, CAP, 8, 128), in_own, in_one, in_two, out_own)


def exchange_kernel(*refs):
    if len(refs) == 7:
        give_ref, half_ref, take_ref, got_ref, sends, recvs, keep = refs
    else:
        give_ref, take_ref, sends, recvs, keep = refs
    c = lax.axis_index("ctx")
    e = lax.axis_index("exp")
    side, z = c % 2, c // 2
    core, x, y = e % 2, (e // 2) % 4, e // 8
    me = e * N_Z + z
    total = N_EXP * N_Z

    def partner(o):
        s, g = o % N_Z, o // N_Z
        dz = jnp.where(s % 2 == 1, (s + 1) // 2, (N_Z - s // 2) % N_Z)
        there = (y + g // 8) % 2 * 8 + (x + (g // 2) % 4) % 4 * 2 + (core + g % 2) % 2
        return there, (z + dz) % N_Z

    def other_half():
        return pltpu.make_async_remote_copy(
            src_ref=half_ref, dst_ref=got_ref, send_sem=sends.at[1], recv_sem=recvs.at[1],
            device_id={"ctx": c + 1 - 2 * side}, device_id_type=pl.DeviceIdType.MESH)

    barrier = pltpu.get_barrier_semaphore()

    def greet(o, _):
        pe, pz = partner(o)
        pl.semaphore_signal(barrier, inc=1, device_id={"exp": pe, "ctx": 2 * pz + side}, device_id_type=pl.DeviceIdType.MESH)
        return 0

    lax.fori_loop(1, total, greet, 0)
    if len(refs) == 7:
        pl.semaphore_signal(barrier, inc=1, device_id={"ctx": c + 1 - 2 * side}, device_id_type=pl.DeviceIdType.MESH)
        pl.semaphore_wait(barrier, total)
        other_half().start()
    else:
        pl.semaphore_wait(barrier, total - 1)

    def send(o, _):
        pe, pz = partner(o)
        pltpu.make_async_remote_copy(
            src_ref=give_ref.at[pe * N_Z + pz], dst_ref=take_ref.at[me], send_sem=sends.at[0], recv_sem=recvs.at[0],
            device_id={"exp": pe, "ctx": 2 * pz + side}, device_id_type=pl.DeviceIdType.MESH).start()
        return 0

    lax.fori_loop(1, total, send, 0)
    stay = pltpu.make_async_copy(give_ref.at[me], take_ref.at[me], keep)
    stay.start()
    stay.wait()
    rest = pltpu.make_async_remote_copy(
        src_ref=give_ref.at[pl.ds(0, total - 1)], dst_ref=take_ref.at[pl.ds(0, total - 1)], send_sem=sends.at[0],
        recv_sem=recvs.at[0], device_id={"ctx": c + 1 - 2 * side}, device_id_type=pl.DeviceIdType.MESH)
    rest.wait_recv()
    rest.wait_send()
    if len(refs) == 7:
        other_half().wait()


def exchanged(blocks, half=None):
    vmem = pl.BlockSpec(memory_space=pltpu.VMEM)
    given = [blocks] if half is None else [blocks, half]
    shapes = [jax.ShapeDtypeStruct(g.shape, g.dtype) for g in given]
    got = pl.pallas_call(
        exchange_kernel,
        out_shape=shapes,
        in_specs=[vmem] * len(given),
        out_specs=[vmem] * len(given),
        scratch_shapes=[pltpu.SemaphoreType.DMA((2,)), pltpu.SemaphoreType.DMA((2,)), pltpu.SemaphoreType.DMA],
        compiler_params=pltpu.CompilerParams(collective_id=4 + len(given), has_side_effects=True, vmem_limit_bytes=24 * 2**20),
        cost_estimate=pl.CostEstimate(flops=0, bytes_accessed=16 * 2**20, transcendentals=0),
        name="dispatch" if half is not None else "giveback",
    )(*given)
    return got


def attention_kernel(q_ref, kv_ref, gain_ref, routing_ref, gate_ref, half_ref, att_ref, rows_ref, spread_ref, got_ref,
                     qs, kv, acc, top, normed, flat, near, sends, recvs, w_sems):
    c = lax.axis_index("ctx")
    side, z = c % 2, c // 2
    mate = c + 1 - 2 * side

    def to(target):
        return dict(device_id={"ctx": target}, device_id_type=pl.DeviceIdType.MESH)

    def ring(way, d, which, block):
        target = jnp.where(way == 0, (z + 1) % N_Z, (z + N_Z - 1) % N_Z) * 2 + side
        return pltpu.make_async_remote_copy(
            src_ref=kv.at[block], dst_ref=kv.at[block], send_sem=sends.at[way, d, which], recv_sem=recvs.at[block], **to(target))

    def arrived(block):
        pltpu.make_async_remote_copy(
            src_ref=kv.at[block], dst_ref=kv.at[block], send_sem=near.at[0], recv_sem=recvs.at[block], **to(mate)).wait_recv()

    pair = pltpu.make_async_remote_copy(
        src_ref=kv.at[c], dst_ref=kv.at[c], send_sem=near.at[0], recv_sem=recvs.at[c], **to(mate))
    weights = pltpu.make_async_remote_copy(
        src_ref=half_ref, dst_ref=got_ref, send_sem=w_sems.at[0], recv_sem=w_sems.at[1], **to(mate))

    barrier = pltpu.get_barrier_semaphore()
    for target in (mate, (z + 1) % N_Z * 2 + side, (z + N_Z - 1) % N_Z * 2 + side):
        pl.semaphore_signal(barrier, inc=1, **to(target))
    kv[c] = kv_ref[...]
    pl.semaphore_wait(barrier, 3)
    pair.start()
    ring(0, 0, 0, c).start()
    ring(1, 0, 0, c).start()

    for h in range(QH):
        qs[pl.ds(h * TOK, TOK), :] = q_ref[:, h * HEAD : (h + 1) * HEAD]

    lanes = lax.broadcasted_iota(jnp.int32, (TOK, 128), 1)
    hit = jnp.zeros((TOK, 128), jnp.float32)
    gates = jnp.zeros((TOK, 128), jnp.float32)
    for k in range(TOP):
        same = (routing_ref[:, k : k + 1] == lanes) & (lanes < EXPERTS)
        hit = jnp.where(same, 1.0, hit)
        gates = jnp.where(same, gate_ref[:, k : k + 1], gates)
    earlier = lax.broadcasted_iota(jnp.int32, (TOK, TOK), 0) > lax.broadcasted_iota(jnp.int32, (TOK, TOK), 1)
    earlier = jnp.where(earlier, 1.0, 0.0).astype(jnp.bfloat16)
    slot = jnp.dot(earlier, hit.astype(jnp.bfloat16), preferred_element_type=jnp.float32)
    expert = lax.broadcasted_iota(jnp.int32, (128, SLOTS), 0)
    column = lax.broadcasted_iota(jnp.int32, (128, SLOTS), 1)
    begin = expert * CAP
    widen = jnp.where((column >= begin) & (column < begin + CAP), 1.0, 0.0).astype(jnp.bfloat16)

    def wide(part):
        return jnp.dot(part.astype(jnp.bfloat16), widen, preferred_element_type=jnp.float32)

    inside = jnp.where((column >= begin) & (column < begin + CAP), column - begin, 0).astype(jnp.float32)
    number = jnp.sum(inside, axis=0, keepdims=True)
    chosen = (wide(hit) > 0.5) & (wide(slot) == number)
    high = gates.astype(jnp.bfloat16).astype(jnp.float32)
    spread_ref[0:TOK, :] = jnp.where(chosen, wide(high), 0.0).astype(jnp.bfloat16)
    spread_ref[TOK : 2 * TOK, :] = jnp.where(chosen, wide(gates - high), 0.0).astype(jnp.bfloat16)
    pick = jnp.where(chosen, 1.0, 0.0).T.astype(jnp.bfloat16)

    arrived(mate)
    ring(0, 0, 1, mate).start()
    ring(1, 0, 1, mate).start()
    weights.start()

    scale = math.log2(math.e) / math.sqrt(HEAD)
    chunk = 2 * TOK

    def attend(zk, diagonal):
        for g in range(KVH):
            keys = kv[pl.ds(2 * zk, 2), :, g * HEAD : (g + 1) * HEAD].reshape(2 * TOK, HEAD)
            vals = kv[pl.ds(2 * zk, 2), :, (KVH + g) * HEAD : (KVH + g + 1) * HEAD].reshape(2 * TOK, HEAD)
            vals = jnp.concatenate([vals, jnp.ones((2 * TOK, HEAD), jnp.bfloat16)], axis=1)

            def rows(n, _):
                here = pl.ds(pl.multiple_of(g * (QH // KVH) * TOK + n * chunk, chunk), chunk)
                score = scale * lax.dot_general(qs[here, :], keys, (((1,), (1,)), ((), ())), preferred_element_type=jnp.float32)
                if diagonal:
                    token = lax.broadcasted_iota(jnp.int32, (chunk, 2 * TOK), 0) % TOK
                    place = lax.broadcasted_iota(jnp.int32, (chunk, 2 * TOK), 1)
                    score = jnp.where(place <= token + TOK * side, score, -1e30)
                    newest = jnp.broadcast_to(jnp.max(score, axis=1, keepdims=True), (chunk, HEAD))
                else:
                    before = top[here, :]
                    newest = jnp.maximum(before, jnp.max(score, axis=1, keepdims=True))
                probs = jnp.exp2(score - jnp.concatenate([newest, newest], axis=1)).astype(jnp.bfloat16)
                made = jnp.dot(probs, vals, preferred_element_type=jnp.float32)
                if not diagonal:
                    keep = jnp.exp2(before - newest)
                    made += acc[here, :] * jnp.concatenate([keep, keep], axis=1)
                acc[here, :] = made
                top[here, :] = newest
                return 0

            lax.fori_loop(0, QH // KVH * TOK // chunk, rows, 0, unroll=2)

    attend(z, True)

    def stage(d, _):
        low, up = (z + N_Z - d) % N_Z, (z + d) % N_Z

        @pl.when(d < 4)
        def _():
            def one(w, _):
                y = (side + w) % 2
                arrived(2 * low + y)

                @pl.when((d < 3) | (y == 0))
                def _():
                    ring(0, d, w, 2 * low + y).start()
                arrived(2 * up + y)

                @pl.when((d < 3) | (y == 1))
                def _():
                    ring(1, d, w, 2 * up + y).start()
                return 0
            lax.fori_loop(0, 2, one, 0)

        @pl.when(d == 4)
        def _():
            arrived(2 * up)
            arrived(2 * up + 1)

        def way(w, _):
            zk = jnp.where(w == 0, low, up)

            @pl.when((zk < z) & ((d < 4) | (w == 0)))
            def _():
                attend(zk, False)
            return 0
        lax.fori_loop(0, 2, way, 0)
        return 0

    lax.fori_loop(1, 5, stage, 0)

    squares = jnp.zeros((TOK, HEAD), jnp.float32)
    for h in range(QH):
        here = pl.ds(h * TOK, TOK)
        out = (acc[here, 0:HEAD] / acc[here, HEAD : 2 * HEAD]).astype(jnp.bfloat16)
        att_ref[:, h * HEAD : (h + 1) * HEAD] = out
        out = out.astype(jnp.float32)
        squares += out * out
    root = lax.rsqrt(jnp.sum(squares, axis=1, keepdims=True) / D + 1e-06)
    for h in range(QH):
        cols = slice(h * HEAD, (h + 1) * HEAD)
        normed[:, cols] = (att_ref[:, cols].astype(jnp.float32) * root * gain_ref[:, cols]).astype(jnp.bfloat16)
    for n in range(4):
        cols = slice(n * PART, (n + 1) * PART)
        picked = jnp.dot(pick, normed[:, cols], preferred_element_type=jnp.float32)
        for k in range(8):
            flat[pl.ds(k, SLOTS, stride=8), :] = picked[:, k * 128 : (k + 1) * 128]
        rows_ref[:, n] = flat[...].astype(jnp.bfloat16).reshape(EXPERTS, CAP, 8, 128)

    pair.wait_send()

    def drain(d, _):
        def one(w, _):
            y = (side + w) % 2

            @pl.when((d < 3) | (y == 0))
            def _():
                ring(0, d, w, c).wait_send()

            @pl.when((d < 3) | (y == 1))
            def _():
                ring(1, d, w, c).wait_send()
            return 0
        return lax.fori_loop(0, 2, one, 0)

    lax.fori_loop(0, 4, drain, 0)
    weights.wait()


def attention(queries, keys_values, gain, routing, gate_weights, half):
    vmem = pl.BlockSpec(memory_space=pltpu.VMEM)
    return pl.pallas_call(
        attention_kernel,
        out_shape=[
            jax.ShapeDtypeStruct((TOK, D), jnp.bfloat16),
            jax.ShapeDtypeStruct((EXPERTS, 4, CAP, 8, 128), jnp.bfloat16),
            jax.ShapeDtypeStruct((2 * TOK, SLOTS), jnp.bfloat16),
            jax.ShapeDtypeStruct(half.shape, half.dtype),
        ],
        in_specs=[vmem] * 6,
        out_specs=[vmem] * 4,
        scratch_shapes=[
            pltpu.VMEM((QH * TOK, HEAD), jnp.bfloat16),
            pltpu.VMEM((2 * N_Z, TOK, 2 * KVH * HEAD), jnp.bfloat16),
            pltpu.VMEM((QH * TOK, 2 * HEAD), jnp.float32),
            pltpu.VMEM((QH * TOK, HEAD), jnp.float32),
            pltpu.VMEM((TOK, D), jnp.bfloat16),
            pltpu.VMEM((8 * SLOTS, 128), jnp.float32),
            pltpu.SemaphoreType.DMA((1,)),
            pltpu.SemaphoreType.DMA((2, 4, 2)),
            pltpu.SemaphoreType.DMA((2 * N_Z,)),
            pltpu.SemaphoreType.DMA((2,)),
        ],
        compiler_params=pltpu.CompilerParams(collective_id=1, has_side_effects=True, vmem_limit_bytes=40 * 2**20),
        cost_estimate=pl.CostEstimate(flops=4 * TOK * 2048 * D, bytes_accessed=8 * 2**20, transcendentals=TOK * 2048 * QH),
        name="attention",
    )(queries, keys_values, gain, routing, gate_weights, half)


def combine_kernel(back_ref, spread_ref, mixed_ref, flat, cols):
    def quarter(n, _):
        flat[...] = back_ref[:, n].astype(jnp.float32).reshape(8 * SLOTS, 128)
        for k in range(8):
            cols[:, k * 128 : (k + 1) * 128] = flat[pl.ds(k, SLOTS, stride=8), :].astype(jnp.bfloat16)
        total = jnp.dot(spread_ref[...], cols[...], preferred_element_type=jnp.float32)
        mixed_ref[:, pl.ds(pl.multiple_of(n * PART, PART), PART)] = (total[:TOK] + total[TOK:]).astype(jnp.bfloat16)
        return 0
    lax.fori_loop(0, 4, quarter, 0)


def combine(back, spread):
    vmem = pl.BlockSpec(memory_space=pltpu.VMEM)
    return pl.pallas_call(
        combine_kernel,
        out_shape=jax.ShapeDtypeStruct((TOK, D), jnp.bfloat16),
        in_specs=[vmem] * 2,
        out_specs=vmem,
        scratch_shapes=[pltpu.VMEM((8 * SLOTS, 128), jnp.float32), pltpu.VMEM((SLOTS, PART), jnp.bfloat16)],
        compiler_params=pltpu.CompilerParams(vmem_limit_bytes=24 * 2**20),
        name="combine",
    )(back, spread)


def local(queries, keys_values, norm_gain, routing, gate_weights, expert_in, expert_out):
    in_own = expert_in[0].reshape(STRIPE, 2 * FF)
    out_own = expert_out[0]
    attended, outgoing, spread, in_one = attention(
        queries[0], keys_values[0], norm_gain[None], routing[0], gate_weights[0], in_own[: STRIPE // 2])
    blocks = (N_EXP * N_Z, CAP, 8, 128)
    rows, in_two = exchanged(outgoing.reshape(blocks), in_own[STRIPE // 2 :])
    made = experts(rows, in_own, in_one, in_two, out_own)
    (back,) = exchanged(made.reshape(blocks))
    mixed = combine(back.reshape(EXPERTS, 4, CAP, 8, 128), spread)
    return (attended[None], mixed[None])


def solution(mesh):
    in_specs = (
        P("exp", "ctx", None),
        P("exp", "ctx", None),
        P(),
        P("exp", "ctx", None),
        P("exp", "ctx", None),
        P(("exp", "ctx"), None, None, None),
        P(("exp", "ctx"), None, None),
    )
    out_specs = (P("exp", "ctx", None), P("exp", "ctx", None))
    return jax.shard_map(local, mesh=mesh, in_specs=in_specs, out_specs=out_specs, check_vma=False)
```

```python
import functools
import math

import jax
import jax.numpy as jnp
from jax import lax
from jax.experimental import pallas as pl
from jax.experimental.pallas import tpu as pltpu
from jax.sharding import PartitionSpec as P

D = 4096
FF = 1536
HEAD = 128
TOP = 8
QH = 32
KVH = 2
GROUP = 8
CAP = 9
EXPERTS = 32
TOK = 128
SLOTS = EXPERTS * CAP
N_EXP = 16
N_Z = 8
ROWS = N_EXP * N_Z * CAP
HALF = ROWS // 2
CHUNK = 16
COUNT = HALF // CHUNK
PACK = 9
BLOCK = CHUNK * PACK
LAG = 2
AHEAD = 4
TILE = 512
PART = D // 4
STRIPE = D // GROUP
GATHER = BLOCK // CAP


def block_kernel(q_ref, kv_ref, gain_ref, routing_ref, gate_ref, in_own, out_own, att_ref, mixed_ref,
                 qs, kv, acc, top, normed, broad, spread, columns, give, take, made_rows, back, in_oth, out_oth, part, recv, hid, flat, xb,
                 near, sends, recvs, w_sems, keep, d_send, d_recv, r_sems, s_send, s_recv, h_send, h_recv):
    c = lax.axis_index("ctx")
    e = lax.axis_index("exp")
    side, z = c % 2, c // 2
    core, x, y = e % 2, (e // 2) % 4, e // 8
    place = z % 4
    home = place * EXPERTS + 2 * e + z // 4
    mate = c + 1 - 2 * side

    def to(target):
        return dict(device_id={"ctx": target}, device_id_type=pl.DeviceIdType.MESH)

    def at(pe, pz):
        return dict(device_id={"exp": pe, "ctx": 2 * pz + side}, device_id_type=pl.DeviceIdType.MESH)

    def ahead(rel):
        return (y + rel // 8) % 2 * 8 + (x + (rel // 2) % 4) % 4 * 2 + (core + rel % 2) % 2

    def behind(rel):
        return (y + rel // 8) % 2 * 8 + (x + 4 - (rel // 2) % 4) % 4 * 2 + (core + rel % 2) % 2

    def turn(u):
        return (z + jnp.where(u % 2 == 1, (u + 1) // 2, N_Z - u // 2)) % N_Z

    def ring(way, d, which, block):
        target = jnp.where(way == 0, (z + 1) % N_Z, (z + N_Z - 1) % N_Z) * 2 + side
        return pltpu.make_async_remote_copy(
            src_ref=kv.at[block], dst_ref=kv.at[block], send_sem=sends.at[way, d, which], recv_sem=recvs.at[block], **to(target))

    def arrived(block):
        pltpu.make_async_remote_copy(
            src_ref=kv.at[block], dst_ref=kv.at[block], send_sem=near.at[0], recv_sem=recvs.at[block], **to(mate)).wait_recv()

    pair = pltpu.make_async_remote_copy(
        src_ref=kv.at[c], dst_ref=kv.at[c], send_sem=near.at[0], recv_sem=recvs.at[c], **to(mate))
    weights = pltpu.make_async_remote_copy(
        src_ref=in_own, dst_ref=in_oth, send_sem=w_sems.at[0], recv_sem=w_sems.at[1], **to(mate))
    down = pltpu.make_async_remote_copy(
        src_ref=out_own, dst_ref=out_oth, send_sem=w_sems.at[2], recv_sem=w_sems.at[3], **to(mate))

    barrier = pltpu.get_barrier_semaphore()
    pl.semaphore_signal(barrier, inc=1, **to(mate))

    def greet(o, _):
        pl.semaphore_signal(barrier, inc=1, **at(ahead(o // N_Z), (z + o) % N_Z))
        return 0

    lax.fori_loop(1, N_EXP * N_Z, greet, 0)
    kv[c] = kv_ref[...]
    pl.semaphore_wait(barrier, N_EXP * N_Z)
    pair.start()
    ring(0, 0, 0, c).start()
    ring(1, 0, 0, c).start()

    for h in range(QH):
        qs[pl.ds(h * TOK, TOK), :] = q_ref[:, h * HEAD : (h + 1) * HEAD]

    lanes = lax.broadcasted_iota(jnp.int32, (TOK, 128), 1)
    hit = jnp.zeros((TOK, 128), jnp.float32)
    gates = jnp.zeros((TOK, 128), jnp.float32)
    lanes = lanes.astype(jnp.float32)
    routes = routing_ref[...].astype(jnp.float32).T
    factors = gate_ref[...].T
    for k in range(TOP):
        same = (routes[:, k : k + 1] == lanes) & (lanes < EXPERTS)
        hit = jnp.where(same, 1.0, hit)
        gates = jnp.where(same, factors[:, k : k + 1], gates)
    earlier = lax.broadcasted_iota(jnp.int32, (TOK, TOK), 0) > lax.broadcasted_iota(jnp.int32, (TOK, TOK), 1)
    earlier = jnp.where(earlier, 1.0, 0.0).astype(jnp.bfloat16)
    slot = jnp.dot(earlier, hit.astype(jnp.bfloat16), preferred_element_type=jnp.float32)
    expert = lax.broadcasted_iota(jnp.int32, (128, SLOTS), 0)
    column = lax.broadcasted_iota(jnp.int32, (128, SLOTS), 1)
    begin = expert * CAP
    widen = jnp.where((column >= begin) & (column < begin + CAP), 1.0, 0.0).astype(jnp.bfloat16)

    def wide(part):
        return jnp.dot(part.astype(jnp.bfloat16), widen, preferred_element_type=jnp.float32)

    inside = jnp.where((column >= begin) & (column < begin + CAP), column - begin, 0).astype(jnp.float32)
    number = jnp.sum(inside, axis=0, keepdims=True)
    chosen = (wide(hit) > 0.5) & (wide(slot) == number)
    high = gates.astype(jnp.bfloat16).astype(jnp.float32)
    spread[0:TOK, :] = jnp.where(chosen, wide(high), 0.0).astype(jnp.bfloat16)
    spread[TOK : 2 * TOK, :] = jnp.where(chosen, wide(gates - high), 0.0).astype(jnp.bfloat16)
    pick = jnp.where(chosen, 1.0, 0.0).T.astype(jnp.bfloat16)

    arrived(mate)
    ring(0, 0, 1, mate).start()
    ring(1, 0, 1, mate).start()
    weights.start()

    scale = math.log2(math.e) / math.sqrt(HEAD)
    chunk = 2 * TOK

    def attend(zk, diagonal):
        for g in range(KVH):
            keys = kv[pl.ds(2 * zk, 2), :, g * HEAD : (g + 1) * HEAD].reshape(2 * TOK, HEAD)
            vals = kv[pl.ds(2 * zk, 2), :, (KVH + g) * HEAD : (KVH + g + 1) * HEAD].reshape(2 * TOK, HEAD)
            vals = jnp.concatenate([vals, jnp.ones((2 * TOK, HEAD), jnp.bfloat16)], axis=1)

            def rows(n, _):
                here = pl.ds(pl.multiple_of(g * (QH // KVH) * TOK + n * chunk, chunk), chunk)
                score = scale * lax.dot_general(qs[here, :], keys, (((1,), (1,)), ((), ())), preferred_element_type=jnp.float32)
                if diagonal:
                    token = lax.broadcasted_iota(jnp.int32, (chunk, 2 * TOK), 0) % TOK
                    place = lax.broadcasted_iota(jnp.int32, (chunk, 2 * TOK), 1)
                    score = jnp.where(place <= token + TOK * side, score, -1e30)
                    newest = jnp.broadcast_to(jnp.max(score, axis=1, keepdims=True), (chunk, HEAD))
                else:
                    before = top[here, :]
                    newest = jnp.maximum(before, jnp.max(score, axis=1, keepdims=True))
                probs = jnp.exp2(score - jnp.concatenate([newest, newest], axis=1)).astype(jnp.bfloat16)
                made = jnp.dot(probs, vals, preferred_element_type=jnp.float32)
                if not diagonal:
                    keep = jnp.exp2(before - newest)
                    made += acc[here, :] * jnp.concatenate([keep, keep], axis=1)
                acc[here, :] = made
                top[here, :] = newest
                return 0

            lax.fori_loop(0, QH // KVH * TOK // chunk, rows, 0, unroll=2)

    attend(z, True)

    def stage(d, _):
        low, up = (z + N_Z - d) % N_Z, (z + d) % N_Z

        @pl.when(d < 4)
        def _():
            def one(w, _):
                v = (side + w) % 2
                arrived(2 * low + v)

                @pl.when((d < 3) | (v == 0))
                def _():
                    ring(0, d, w, 2 * low + v).start()
                arrived(2 * up + v)

                @pl.when((d < 3) | (v == 1))
                def _():
                    ring(1, d, w, 2 * up + v).start()
                return 0
            lax.fori_loop(0, 2, one, 0)

        @pl.when(d == 4)
        def _():
            arrived(2 * up)
            arrived(2 * up + 1)

        def way(w, _):
            zk = jnp.where(w == 0, low, up)

            @pl.when((zk < z) & ((d < 4) | (w == 0)))
            def _():
                attend(zk, False)
            return 0
        lax.fori_loop(0, 2, way, 0)
        return 0

    lax.fori_loop(1, 5, stage, 0)

    squares = jnp.zeros((TOK, HEAD), jnp.float32)
    for h in range(QH):
        here = pl.ds(h * TOK, TOK)
        out = (acc[here, 0:HEAD] / acc[here, HEAD : 2 * HEAD]).astype(jnp.bfloat16)
        att_ref[:, h * HEAD : (h + 1) * HEAD] = out
        out = out.astype(jnp.float32)
        squares += out * out
    root = lax.rsqrt(jnp.sum(squares, axis=1, keepdims=True) / D + 1e-06)
    for h in range(QH):
        cols = slice(h * HEAD, (h + 1) * HEAD)
        normed[:, cols] = (att_ref[:, cols].astype(jnp.float32) * root * gain_ref[:, cols]).astype(jnp.bfloat16)
    for n in range(4):
        cols = slice(n * PART, (n + 1) * PART)
        picked = jnp.dot(pick, normed[:, cols], preferred_element_type=jnp.float32)
        for k in range(8):
            broad[pl.ds(k, SLOTS, stride=8), :] = picked[:, k * 128 : (k + 1) * 128]
        give[n * EXPERTS : (n + 1) * EXPERTS] = broad[...].astype(jnp.bfloat16).reshape(EXPERTS, CAP, 8, 128)

    own = pl.ds(pl.multiple_of(side * STRIPE, STRIPE), STRIPE)
    oth = pl.ds(pl.multiple_of((1 - side) * STRIPE, STRIPE), STRIPE)

    def sum_copy(d, i):
        target = jnp.where(d == 1, c + 2, c - 2)
        return pltpu.make_async_remote_copy(
            src_ref=part.at[d, i], dst_ref=recv.at[d, i], send_sem=s_send.at[d, i], recv_sem=s_recv.at[d, i],
            device_id={"ctx": target}, device_id_type=pl.DeviceIdType.MESH)

    def hid_copy(d, i):
        target = jnp.where(d == 1, c - 2, c + 2)
        return pltpu.make_async_remote_copy(
            src_ref=hid.at[d, i], dst_ref=hid.at[d, i], send_sem=h_send.at[d, i], recv_sem=h_recv.at[d, i],
            device_id={"ctx": target}, device_id_type=pl.DeviceIdType.MESH)

    def products(d, b):
        flat[...] = take[d, b].astype(jnp.float32).reshape(8 * BLOCK, 128)
        for k in range(8):
            xb[:, k * 128 : (k + 1) * 128] = flat[pl.ds(k, BLOCK, stride=8), :].astype(jnp.bfloat16)

        def tile(n, _):
            cols = pl.ds(pl.multiple_of(n * TILE, TILE), TILE)
            made = jnp.dot(xb[:, own], in_own[:, cols], preferred_element_type=jnp.float32)
            made += jnp.dot(xb[:, oth], in_oth[:, cols], preferred_element_type=jnp.float32)
            part[d, pl.ds(b * PACK, PACK), :, cols] = made.astype(jnp.bfloat16).reshape(PACK, CHUNK, TILE)
            return 0
        lax.fori_loop(0, 2 * FF // TILE, tile, 0)

    def result(d, b):
        rows = hid[d, pl.ds(b * PACK, PACK)].reshape(BLOCK, FF)
        mine = jnp.dot(rows, out_own[...], preferred_element_type=jnp.float32)
        theirs = jnp.dot(rows, out_oth[...], preferred_element_type=jnp.float32)
        for k in range(4):
            cols = slice(k * 128, (k + 1) * 128)
            flat[pl.ds(k, BLOCK, stride=8), :] = jnp.where(side == 0, mine[:, cols], theirs[:, cols])
            flat[pl.ds(k + 4, BLOCK, stride=8), :] = jnp.where(side == 0, theirs[:, cols], mine[:, cols])
        made_rows[d, b] = flat[...].astype(jnp.bfloat16).reshape(GATHER, CAP, 8, 128)

        def back_home(j, _):
            low, s = j // N_Z, turn(j % N_Z)
            rel = d * 8 + 2 * b + low
            local = (rel == 0) & (j == 0)

            @pl.when(local)
            def _():
                pltpu.make_async_copy(made_rows.at[0, 0, z], back.at[home], keep.at[1]).start()

            @pl.when(jnp.logical_not(local))
            def _():
                pltpu.make_async_remote_copy(
                    src_ref=made_rows.at[d, b, low * N_Z + s], dst_ref=back.at[home], send_sem=r_sems.at[0], recv_sem=r_sems.at[1],
                    **at(behind(rel), s)).start()
            return 0

        lax.fori_loop(0, GATHER, back_home, 0)

    def dispatch(b, u):
        pz = turn(u)

        def one(v, _):
            d, low = v % 2, v // 2
            rel = d * 8 + 2 * b + low
            pe = ahead(rel)
            local = (rel == 0) & (u == 0)

            @pl.when(local)
            def _():
                pltpu.make_async_copy(give.at[home], take.at[0, 0, z], keep.at[0]).start()

            @pl.when(jnp.logical_not(local))
            def _():
                pltpu.make_async_remote_copy(
                    src_ref=give.at[pz % 4 * EXPERTS + 2 * pe + pz // 4], dst_ref=take.at[d, b, low * N_Z + z],
                    send_sem=d_send.at[0], recv_sem=d_recv.at[d, b], **at(pe, pz)).start()
            return 0

        lax.fori_loop(0, 4, one, 0)

    def ahead_of_time(n, _):
        dispatch(n // N_Z, n % N_Z)
        return 0

    lax.fori_loop(0, AHEAD * N_Z, ahead_of_time, 0)
    down.start()

    def await_rows(d, b, count):
        pltpu.make_async_remote_copy(
            src_ref=take.at[d, b, pl.ds(0, count)], dst_ref=take.at[d, b, pl.ds(0, count)], send_sem=d_send.at[0],
            recv_sem=d_recv.at[d, b], **to(mate)).wait_recv()

    def step(t, _):
        @pl.when((t // PACK + AHEAD < COUNT // PACK) & (t % PACK < N_Z))
        def _():
            dispatch(t // PACK + AHEAD, t % PACK)

        @pl.when((t % PACK == 0) & (t < COUNT))
        def _():
            @pl.when(t == 0)
            def _():
                weights.wait_recv()
                pltpu.make_async_copy(give.at[home], take.at[0, 0, z], keep.at[0]).wait()
                await_rows(0, 0, GATHER - 1)

            @pl.when(t > 0)
            def _():
                await_rows(0, t // PACK, GATHER)

            def both(d, _):
                @pl.when(d == 1)
                def _():
                    await_rows(1, t // PACK, GATHER)
                products(d, t // PACK)
                return 0
            lax.fori_loop(0, 2, both, 0)

        @pl.when(t == 3 * LAG + PACK - 1)
        def _():
            down.wait_recv()

        def direction(d, _):
            pos = jnp.where(d == 1, place, 3 - place)
            i = t - LAG * pos

            @pl.when((i >= 0) & (i < COUNT))
            def _():
                @pl.when(pos == 0)
                def _():
                    sum_copy(d, i).start()

                @pl.when((pos > 0) & (pos < 3))
                def _():
                    sum_copy(d, i).wait_recv()
                    part[d, i] = (part[d, i].astype(jnp.float32) + recv[d, i].astype(jnp.float32)).astype(jnp.bfloat16)
                    sum_copy(d, i).start()

                @pl.when(pos == 3)
                def _():
                    sum_copy(d, i).wait_recv()
                    total = part[d, i].astype(jnp.float32) + recv[d, i].astype(jnp.float32)
                    gate = total[:, :FF]
                    hid[d, i] = (jax.nn.silu(gate) * total[:, FF:]).astype(jnp.bfloat16)
                    hid_copy(d, i).start()

            k = t - 3 * LAG - LAG * (3 - pos)

            @pl.when((k >= 0) & (k < COUNT))
            def _():
                @pl.when(pos < 3)
                def _():
                    hid_copy(d, k).wait_recv()

                @pl.when((pos > 0) & (pos < 3))
                def _():
                    hid_copy(d, k).start()

                @pl.when(k % PACK == PACK - 1)
                def _():
                    result(d, k // PACK)
            return 0

        lax.fori_loop(0, 2, direction, 0)
        return 0

    lax.fori_loop(0, COUNT + 6 * LAG, step, 0)

    def drain(i, _):
        def direction(d, _):
            pos = jnp.where(d == 1, place, 3 - place)

            @pl.when(pos < 3)
            def _():
                sum_copy(d, i).wait_send()

            @pl.when(pos > 0)
            def _():
                hid_copy(d, i).wait_send()
            return 0
        lax.fori_loop(0, 2, direction, 0)
        return 0

    lax.fori_loop(0, COUNT, drain, 0)
    weights.wait_send()
    down.wait_send()
    pltpu.make_async_copy(made_rows.at[0, 0, z], back.at[home], keep.at[1]).wait()
    others = pl.ds(0, N_EXP * N_Z - 1)
    pltpu.make_async_remote_copy(
        src_ref=give.at[others], dst_ref=back.at[others], send_sem=d_send.at[0], recv_sem=r_sems.at[1], **to(mate)).wait_send()
    returned = pltpu.make_async_remote_copy(
        src_ref=back.at[others], dst_ref=back.at[others], send_sem=r_sems.at[0], recv_sem=r_sems.at[1], **to(mate))
    returned.wait_send()
    returned.wait_recv()

    def quarter(n, _):
        broad[...] = back[pl.ds(n * EXPERTS, EXPERTS)].astype(jnp.float32).reshape(8 * SLOTS, 128)
        for k in range(8):
            columns[:, k * 128 : (k + 1) * 128] = broad[pl.ds(k, SLOTS, stride=8), :].astype(jnp.bfloat16)
        total = jnp.dot(spread[...], columns[...], preferred_element_type=jnp.float32)
        mixed_ref[:, pl.ds(pl.multiple_of(n * PART, PART), PART)] = (total[:TOK] + total[TOK:]).astype(jnp.bfloat16)
        return 0

    lax.fori_loop(0, 4, quarter, 0)

    pair.wait_send()

    def drain(d, _):
        def one(w, _):
            v = (side + w) % 2

            @pl.when((d < 3) | (v == 0))
            def _():
                ring(0, d, w, c).wait_send()

            @pl.when((d < 3) | (v == 1))
            def _():
                ring(1, d, w, c).wait_send()
            return 0
        return lax.fori_loop(0, 2, one, 0)

    lax.fori_loop(0, 4, drain, 0)


def block(queries, keys_values, gain, routing, gate_weights, in_own, out_own):
    vmem = pl.BlockSpec(memory_space=pltpu.VMEM)
    blocks = (N_EXP * N_Z, CAP, 8, 128)
    grouped = (2, COUNT // PACK, GATHER, CAP, 8, 128)
    bf16 = jnp.bfloat16
    return pl.pallas_call(
        block_kernel,
        out_shape=[jax.ShapeDtypeStruct((TOK, D), bf16), jax.ShapeDtypeStruct((TOK, D), bf16)],
        in_specs=[vmem] * 7,
        out_specs=[vmem] * 2,
        scratch_shapes=[
            pltpu.VMEM((QH * TOK, HEAD), bf16),
            pltpu.VMEM((2 * N_Z, TOK, 2 * KVH * HEAD), bf16),
            pltpu.VMEM((QH * TOK, 2 * HEAD), jnp.float32),
            pltpu.VMEM((QH * TOK, HEAD), jnp.float32),
            pltpu.VMEM((TOK, D), bf16),
            pltpu.VMEM((8 * SLOTS, 128), jnp.float32),
            pltpu.VMEM((2 * TOK, SLOTS), bf16),
            pltpu.VMEM((SLOTS, PART), bf16),
            pltpu.VMEM(blocks, bf16),
            pltpu.VMEM(grouped, bf16),
            pltpu.VMEM(grouped, bf16),
            pltpu.VMEM(blocks, bf16),
            pltpu.VMEM((STRIPE, 2 * FF), bf16),
            pltpu.VMEM((FF, STRIPE), bf16),
            pltpu.VMEM((2, COUNT, CHUNK, 2 * FF), bf16),
            pltpu.VMEM((2, COUNT, CHUNK, 2 * FF), bf16),
            pltpu.VMEM((2, COUNT, CHUNK, FF), bf16),
            pltpu.VMEM((8 * BLOCK, 128), jnp.float32),
            pltpu.VMEM((BLOCK, PART), bf16),
            pltpu.SemaphoreType.DMA((1,)),
            pltpu.SemaphoreType.DMA((2, 4, 2)),
            pltpu.SemaphoreType.DMA((2 * N_Z,)),
            pltpu.SemaphoreType.DMA((4,)),
            pltpu.SemaphoreType.DMA((2,)),
            pltpu.SemaphoreType.DMA((1,)),
            pltpu.SemaphoreType.DMA((2, COUNT // PACK)),
            pltpu.SemaphoreType.DMA((2,)),
            pltpu.SemaphoreType.DMA((2, COUNT)),
            pltpu.SemaphoreType.DMA((2, COUNT)),
            pltpu.SemaphoreType.DMA((2, COUNT)),
            pltpu.SemaphoreType.DMA((2, COUNT)),
        ],
        compiler_params=pltpu.CompilerParams(collective_id=1, has_side_effects=True, vmem_limit_bytes=60 * 2**20),
        cost_estimate=pl.CostEstimate(flops=26 * 10**9, bytes_accessed=12 * 2**20, transcendentals=TOK * 2048 * QH),
        name="block",
    )(queries, keys_values, gain, routing, gate_weights, in_own, out_own)


def local(queries, keys_values, norm_gain, routing, gate_weights, expert_in, expert_out):
    in_own = expert_in[0].reshape(STRIPE, 2 * FF)
    attended, mixed = block(
        queries[0], keys_values[0], norm_gain[None], routing[0].T, gate_weights[0].T, in_own, expert_out[0])
    return (attended[None], mixed[None])


def solution(mesh):
    in_specs = (
        P("exp", "ctx", None),
        P("exp", "ctx", None),
        P(),
        P("exp", "ctx", None),
        P("exp", "ctx", None),
        P(("exp", "ctx"), None, None, None),
        P(("exp", "ctx"), None, None),
    )
    out_specs = (P("exp", "ctx", None), P("exp", "ctx", None))
    return jax.shard_map(local, mesh=mesh, in_specs=in_specs, out_specs=out_specs, check_vma=False)
```

```python
import functools
import math

import jax
import jax.numpy as jnp
from jax import lax
from jax.experimental import pallas as pl
from jax.experimental.pallas import tpu as pltpu
from jax.sharding import PartitionSpec as P

D = 4096
FF = 1536
HEAD = 128
TOP = 8
QH = 32
KVH = 2
GROUP = 8
CAP = 9
EXPERTS = 32
TOK = 128
SLOTS = EXPERTS * CAP
N_EXP = 16
N_Z = 8
ROWS = N_EXP * N_Z * CAP
HALF = ROWS // 2
CHUNK = 16
COUNT = HALF // CHUNK
PACK = 9
BLOCK = CHUNK * PACK
LAG = 2
BACK_LAG = 2
AHEAD = 4
TILE = 512
PART = D // 4
STRIPE = D // GROUP
GATHER = BLOCK // CAP


def block_kernel(q_ref, kv_ref, gain_ref, routing_ref, gate_ref, in_own, out_own, att_ref, back, spread,
                 qs, kv, acc, top, normed, broad, give, take, made_rows, in_oth, out_oth, part, recv, hid, flat, xb,
                 near, sends, recvs, w_sems, keep, d_send, d_recv, r_sems, s_send, s_recv, h_send, h_recv):
    c = lax.axis_index("ctx")
    e = lax.axis_index("exp")
    side, z = c % 2, c // 2
    core, x, y = e % 2, (e // 2) % 4, e // 8
    place = z % 4
    home = place * EXPERTS + 2 * e + z // 4
    mate = c + 1 - 2 * side

    def to(target):
        return dict(device_id={"ctx": target}, device_id_type=pl.DeviceIdType.MESH)

    def at(pe, pz):
        return dict(device_id={"exp": pe, "ctx": 2 * pz + side}, device_id_type=pl.DeviceIdType.MESH)

    def ahead(rel):
        return (y + rel // 8) % 2 * 8 + (x + (rel // 2 + rel // 8 + rel % 2 * 2) % 4) % 4 * 2 + (core + rel % 2) % 2

    def behind(rel):
        return (y + rel // 8) % 2 * 8 + (x + 4 - (rel // 2 + rel // 8 + rel % 2 * 2) % 4) % 4 * 2 + (core + rel % 2) % 2

    def turn(u):
        return (z + jnp.where(u % 2 == 1, (u + 1) // 2, N_Z - u // 2)) % N_Z

    def ring(way, d, which, block):
        target = jnp.where(way == 0, (z + 1) % N_Z, (z + N_Z - 1) % N_Z) * 2 + side
        return pltpu.make_async_remote_copy(
            src_ref=kv.at[block], dst_ref=kv.at[block], send_sem=sends.at[way, d, which], recv_sem=recvs.at[block], **to(target))

    def arrived(block):
        pltpu.make_async_remote_copy(
            src_ref=kv.at[block], dst_ref=kv.at[block], send_sem=near.at[0], recv_sem=recvs.at[block], **to(mate)).wait_recv()

    pair = pltpu.make_async_remote_copy(
        src_ref=kv.at[c], dst_ref=kv.at[c], send_sem=near.at[0], recv_sem=recvs.at[c], **to(mate))
    weights = pltpu.make_async_remote_copy(
        src_ref=in_own, dst_ref=in_oth, send_sem=w_sems.at[0], recv_sem=w_sems.at[1], **to(mate))
    down = pltpu.make_async_remote_copy(
        src_ref=out_own, dst_ref=out_oth, send_sem=w_sems.at[2], recv_sem=w_sems.at[3], **to(mate))

    barrier = pltpu.get_barrier_semaphore()
    pl.semaphore_signal(barrier, inc=1, **to(mate))

    def greet(o, _):
        pl.semaphore_signal(barrier, inc=1, **at(ahead(o // N_Z), (z + o) % N_Z))
        return 0

    lax.fori_loop(1, N_EXP * N_Z, greet, 0)
    kv[c] = kv_ref[...]
    pl.semaphore_wait(barrier, N_EXP * N_Z)
    pair.start()
    ring(0, 0, 0, c).start()
    ring(1, 0, 0, c).start()
    weights.start()

    for h in range(QH):
        qs[pl.ds(h * TOK, TOK), :] = q_ref[:, h * HEAD : (h + 1) * HEAD]

    lanes = lax.broadcasted_iota(jnp.int32, (TOK, 128), 1)
    hit = jnp.zeros((TOK, 128), jnp.float32)
    gates = jnp.zeros((TOK, 128), jnp.float32)
    lanes = lanes.astype(jnp.float32)
    routes = routing_ref[...].astype(jnp.float32).T
    factors = gate_ref[...].T
    for k in range(TOP):
        same = (routes[:, k : k + 1] == lanes) & (lanes < EXPERTS)
        hit = jnp.where(same, 1.0, hit)
        gates = jnp.where(same, factors[:, k : k + 1], gates)
    earlier = lax.broadcasted_iota(jnp.int32, (TOK, TOK), 0) > lax.broadcasted_iota(jnp.int32, (TOK, TOK), 1)
    earlier = jnp.where(earlier, 1.0, 0.0).astype(jnp.bfloat16)
    slot = jnp.dot(earlier, hit.astype(jnp.bfloat16), preferred_element_type=jnp.float32)
    expert = lax.broadcasted_iota(jnp.int32, (128, SLOTS), 0)
    column = lax.broadcasted_iota(jnp.int32, (128, SLOTS), 1)
    begin = expert * CAP
    widen = jnp.where((column >= begin) & (column < begin + CAP), 1.0, 0.0).astype(jnp.bfloat16)

    def wide(part):
        return jnp.dot(part.astype(jnp.bfloat16), widen, preferred_element_type=jnp.float32)

    inside = jnp.where((column >= begin) & (column < begin + CAP), column - begin, 0).astype(jnp.float32)
    number = jnp.sum(inside, axis=0, keepdims=True)
    chosen = (wide(hit) > 0.5) & (wide(slot) == number)
    high = gates.astype(jnp.bfloat16).astype(jnp.float32)
    spread[0:TOK, :] = jnp.where(chosen, wide(high), 0.0).astype(jnp.bfloat16)
    spread[TOK : 2 * TOK, :] = jnp.where(chosen, wide(gates - high), 0.0).astype(jnp.bfloat16)
    pick = jnp.where(chosen, 1.0, 0.0).T.astype(jnp.bfloat16)

    arrived(mate)
    ring(0, 0, 1, mate).start()
    ring(1, 0, 1, mate).start()

    scale = math.log2(math.e) / math.sqrt(HEAD)
    chunk = 2 * TOK

    def attend(zk, diagonal):
        for g in range(KVH):
            keys = kv[pl.ds(2 * zk, 2), :, g * HEAD : (g + 1) * HEAD].reshape(2 * TOK, HEAD)
            vals = kv[pl.ds(2 * zk, 2), :, (KVH + g) * HEAD : (KVH + g + 1) * HEAD].reshape(2 * TOK, HEAD)
            vals = jnp.concatenate([vals, jnp.ones((2 * TOK, HEAD), jnp.bfloat16)], axis=1)

            def rows(n, _):
                here = pl.ds(pl.multiple_of(g * (QH // KVH) * TOK + n * chunk, chunk), chunk)
                score = scale * lax.dot_general(qs[here, :], keys, (((1,), (1,)), ((), ())), preferred_element_type=jnp.float32)
                if diagonal:
                    token = lax.broadcasted_iota(jnp.int32, (chunk, 2 * TOK), 0) % TOK
                    place = lax.broadcasted_iota(jnp.int32, (chunk, 2 * TOK), 1)
                    score = jnp.where(place <= token + TOK * side, score, -1e30)
                    newest = jnp.broadcast_to(jnp.max(score, axis=1, keepdims=True), (chunk, HEAD))
                else:
                    before = top[here, :]
                    newest = jnp.maximum(before, jnp.max(score, axis=1, keepdims=True))
                probs = jnp.exp2(score - jnp.concatenate([newest, newest], axis=1)).astype(jnp.bfloat16)
                made = jnp.dot(probs, vals, preferred_element_type=jnp.float32)
                if not diagonal:
                    keep = jnp.exp2(before - newest)
                    made += acc[here, :] * jnp.concatenate([keep, keep], axis=1)
                acc[here, :] = made
                top[here, :] = newest
                return 0

            lax.fori_loop(0, QH // KVH * TOK // chunk, rows, 0, unroll=2)

    attend(z, True)

    def finish():
        squares = jnp.zeros((TOK, HEAD), jnp.float32)
        for h in range(QH):
            here = pl.ds(h * TOK, TOK)
            out = (acc[here, 0:HEAD] / acc[here, HEAD : 2 * HEAD]).astype(jnp.bfloat16)
            att_ref[:, h * HEAD : (h + 1) * HEAD] = out
            out = out.astype(jnp.float32)
            squares += out * out
        root = lax.rsqrt(jnp.sum(squares, axis=1, keepdims=True) / D + 1e-06)
        for h in range(QH):
            cols = slice(h * HEAD, (h + 1) * HEAD)
            normed[:, cols] = (att_ref[:, cols].astype(jnp.float32) * root * gain_ref[:, cols]).astype(jnp.bfloat16)
        for n in range(4):
            cols = slice(n * PART, (n + 1) * PART)
            picked = jnp.dot(pick, normed[:, cols], preferred_element_type=jnp.float32)
            for k in range(8):
                broad[pl.ds(k, SLOTS, stride=8), :] = picked[:, k * 128 : (k + 1) * 128]
            give[n * EXPERTS : (n + 1) * EXPERTS] = broad[...].astype(jnp.bfloat16).reshape(EXPERTS, CAP, 8, 128)

    def dispatch(b, u):
        pz = turn(u)

        def one(v, _):
            d, low = v % 2, v // 2
            rel = d * 8 + 2 * b + low
            pe = ahead(rel)
            local = (rel == 0) & (u == 0)

            @pl.when(local)
            def _():
                pltpu.make_async_copy(give.at[home], take.at[0, 0, z], keep.at[0]).start()

            @pl.when(jnp.logical_not(local))
            def _():
                pltpu.make_async_remote_copy(
                    src_ref=give.at[pz % 4 * EXPERTS + 2 * pe + pz // 4], dst_ref=take.at[d, b, low * N_Z + z],
                    send_sem=d_send.at[0], recv_sem=d_recv.at[d, b], **at(pe, pz)).start()
            return 0

        lax.fori_loop(0, 4, one, 0)

    def ahead_of_time(n, _):
        dispatch(n // N_Z, n % N_Z)
        return 0

    def stage(d, _):
        low, up = (z + N_Z - d) % N_Z, (z + d) % N_Z

        @pl.when(d < 4)
        def _():
            def one(w, _):
                v = (side + w) % 2
                arrived(2 * low + v)

                @pl.when((d < 3) | (v == 0))
                def _():
                    ring(0, d, w, 2 * low + v).start()
                arrived(2 * up + v)

                @pl.when((d < 3) | (v == 1))
                def _():
                    ring(1, d, w, 2 * up + v).start()
                return 0
            lax.fori_loop(0, 2, one, 0)

        @pl.when(d == 4)
        def _():
            arrived(2 * up)
            arrived(2 * up + 1)

        def way(w, _):
            zk = jnp.where(w == 0, low, up)

            @pl.when((zk < z) & ((d < 4) | (w == 0)))
            def _():
                attend(zk, False)
            return 0
        lax.fori_loop(0, 2, way, 0)

        @pl.when(d == 4)
        def _():
            finish()

        @pl.when(d == 4)
        def _():
            lax.fori_loop(0, AHEAD * N_Z, ahead_of_time, 0)
        return 0

    lax.fori_loop(1, 5, stage, 0)
    down.start()

    own = pl.ds(pl.multiple_of(side * STRIPE, STRIPE), STRIPE)
    oth = pl.ds(pl.multiple_of((1 - side) * STRIPE, STRIPE), STRIPE)

    def sum_copy(d, i):
        target = jnp.where(d == 1, c + 2, c - 2)
        return pltpu.make_async_remote_copy(
            src_ref=part.at[d, i], dst_ref=recv.at[d, i], send_sem=s_send.at[d, i], recv_sem=s_recv.at[d, i],
            device_id={"ctx": target}, device_id_type=pl.DeviceIdType.MESH)

    def hid_copy(d, i):
        target = jnp.where(d == 1, c - 2, c + 2)
        return pltpu.make_async_remote_copy(
            src_ref=hid.at[d, i], dst_ref=hid.at[d, i], send_sem=h_send.at[d, i], recv_sem=h_recv.at[d, i],
            device_id={"ctx": target}, device_id_type=pl.DeviceIdType.MESH)

    def products(d, b):
        flat[...] = take[d, b].astype(jnp.float32).reshape(8 * BLOCK, 128)
        for k in range(8):
            xb[:, k * 128 : (k + 1) * 128] = flat[pl.ds(k, BLOCK, stride=8), :].astype(jnp.bfloat16)

        def tile(n, _):
            cols = pl.ds(pl.multiple_of(n * TILE, TILE), TILE)
            made = jnp.dot(xb[:, own], in_own[:, cols], preferred_element_type=jnp.float32)
            made += jnp.dot(xb[:, oth], in_oth[:, cols], preferred_element_type=jnp.float32)
            part[d, pl.ds(b * PACK, PACK), :, cols] = made.astype(jnp.bfloat16).reshape(PACK, CHUNK, TILE)
            return 0
        lax.fori_loop(0, 2 * FF // TILE, tile, 0)

    def result(d, b):
        rows = hid[d, pl.ds(b * PACK, PACK)].reshape(BLOCK, FF)
        mine = jnp.dot(rows, out_own[...], preferred_element_type=jnp.float32)
        theirs = jnp.dot(rows, out_oth[...], preferred_element_type=jnp.float32)
        for k in range(4):
            cols = slice(k * 128, (k + 1) * 128)
            flat[pl.ds(k, BLOCK, stride=8), :] = jnp.where(side == 0, mine[:, cols], theirs[:, cols])
            flat[pl.ds(k + 4, BLOCK, stride=8), :] = jnp.where(side == 0, theirs[:, cols], mine[:, cols])
        made_rows[d, b] = flat[...].astype(jnp.bfloat16).reshape(GATHER, CAP, 8, 128)

        def back_home(j, _):
            low, s = j // N_Z, turn(j % N_Z)
            rel = d * 8 + 2 * b + low
            local = (rel == 0) & (j == 0)

            @pl.when(local)
            def _():
                pltpu.make_async_copy(made_rows.at[0, 0, z], back.at[home], keep.at[1]).start()

            @pl.when(jnp.logical_not(local))
            def _():
                pltpu.make_async_remote_copy(
                    src_ref=made_rows.at[d, b, low * N_Z + s], dst_ref=back.at[home], send_sem=r_sems.at[0], recv_sem=r_sems.at[1],
                    **at(behind(rel), s)).start()
            return 0

        lax.fori_loop(0, GATHER, back_home, 0)

    def await_rows(d, b, count):
        pltpu.make_async_remote_copy(
            src_ref=take.at[d, b, pl.ds(0, count)], dst_ref=take.at[d, b, pl.ds(0, count)], send_sem=d_send.at[0],
            recv_sem=d_recv.at[d, b], **to(mate)).wait_recv()

    def step(t, _):
        @pl.when((t // PACK + AHEAD < COUNT // PACK) & (t % PACK < N_Z))
        def _():
            dispatch(t // PACK + AHEAD, t % PACK)

        @pl.when((t % PACK == 0) & (t < COUNT))
        def _():
            @pl.when(t == 0)
            def _():
                weights.wait_recv()
                pltpu.make_async_copy(give.at[home], take.at[0, 0, z], keep.at[0]).wait()
                await_rows(0, 0, GATHER - 1)

            @pl.when(t > 0)
            def _():
                await_rows(0, t // PACK, GATHER)

            def both(d, _):
                @pl.when(d == 1)
                def _():
                    await_rows(1, t // PACK, GATHER)
                products(d, t // PACK)
                return 0
            lax.fori_loop(0, 2, both, 0)

        @pl.when(t == 3 * LAG + PACK - 1)
        def _():
            down.wait_recv()

        def direction(d, _):
            pos = jnp.where(d == 1, place, 3 - place)
            i = t - LAG * pos

            @pl.when((i >= 0) & (i < COUNT))
            def _():
                @pl.when(pos == 0)
                def _():
                    sum_copy(d, i).start()

                @pl.when((pos > 0) & (pos < 3))
                def _():
                    sum_copy(d, i).wait_recv()
                    part[d, i] = (part[d, i].astype(jnp.float32) + recv[d, i].astype(jnp.float32)).astype(jnp.bfloat16)
                    sum_copy(d, i).start()

                @pl.when(pos == 3)
                def _():
                    sum_copy(d, i).wait_recv()
                    total = part[d, i].astype(jnp.float32) + recv[d, i].astype(jnp.float32)
                    gate = total[:, :FF]
                    hid[d, i] = (jax.nn.silu(gate) * total[:, FF:]).astype(jnp.bfloat16)
                    hid_copy(d, i).start()

            k = t - 3 * LAG - BACK_LAG * (3 - pos)

            @pl.when((k >= 0) & (k < COUNT))
            def _():
                @pl.when(pos < 3)
                def _():
                    hid_copy(d, k).wait_recv()

                @pl.when((pos > 0) & (pos < 3))
                def _():
                    hid_copy(d, k).start()

                @pl.when(k % PACK == PACK - 1)
                def _():
                    result(d, k // PACK)
            return 0

        lax.fori_loop(0, 2, direction, 0)
        return 0

    lax.fori_loop(0, COUNT + 3 * LAG + 3 * BACK_LAG, step, 0)

    def drain(i, _):
        def direction(d, _):
            pos = jnp.where(d == 1, place, 3 - place)

            @pl.when(pos < 3)
            def _():
                sum_copy(d, i).wait_send()

            @pl.when(pos > 0)
            def _():
                hid_copy(d, i).wait_send()
            return 0
        lax.fori_loop(0, 2, direction, 0)
        return 0

    lax.fori_loop(0, COUNT, drain, 0)
    weights.wait_send()
    down.wait_send()
    pltpu.make_async_copy(made_rows.at[0, 0, z], back.at[home], keep.at[1]).wait()
    others = pl.ds(0, N_EXP * N_Z - 1)
    pltpu.make_async_remote_copy(
        src_ref=give.at[others], dst_ref=back.at[others], send_sem=d_send.at[0], recv_sem=r_sems.at[1], **to(mate)).wait_send()
    returned = pltpu.make_async_remote_copy(
        src_ref=back.at[others], dst_ref=back.at[others], send_sem=r_sems.at[0], recv_sem=r_sems.at[1], **to(mate))
    returned.wait_send()
    returned.wait_recv()

    pair.wait_send()

    def drain(d, _):
        def one(w, _):
            v = (side + w) % 2

            @pl.when((d < 3) | (v == 0))
            def _():
                ring(0, d, w, c).wait_send()

            @pl.when((d < 3) | (v == 1))
            def _():
                ring(1, d, w, c).wait_send()
            return 0
        return lax.fori_loop(0, 2, one, 0)

    lax.fori_loop(0, 4, drain, 0)


def block(queries, keys_values, gain, routing, gate_weights, in_own, out_own):
    vmem = pl.BlockSpec(memory_space=pltpu.VMEM)
    blocks = (N_EXP * N_Z, CAP, 8, 128)
    grouped = (2, COUNT // PACK, GATHER, CAP, 8, 128)
    bf16 = jnp.bfloat16
    return pl.pallas_call(
        block_kernel,
        out_shape=[
            jax.ShapeDtypeStruct((TOK, D), bf16),
            jax.ShapeDtypeStruct(blocks, bf16),
            jax.ShapeDtypeStruct((2 * TOK, SLOTS), bf16),
        ],
        in_specs=[vmem] * 7,
        out_specs=[vmem] * 3,
        scratch_shapes=[
            pltpu.VMEM((QH * TOK, HEAD), bf16),
            pltpu.VMEM((2 * N_Z, TOK, 2 * KVH * HEAD), bf16),
            pltpu.VMEM((QH * TOK, 2 * HEAD), jnp.float32),
            pltpu.VMEM((QH * TOK, HEAD), jnp.float32),
            pltpu.VMEM((TOK, D), bf16),
            pltpu.VMEM((8 * SLOTS, 128), jnp.float32),
            pltpu.VMEM(blocks, bf16),
            pltpu.VMEM(grouped, bf16),
            pltpu.VMEM(grouped, bf16),
            pltpu.VMEM((STRIPE, 2 * FF), bf16),
            pltpu.VMEM((FF, STRIPE), bf16),
            pltpu.VMEM((2, COUNT, CHUNK, 2 * FF), bf16),
            pltpu.VMEM((2, COUNT, CHUNK, 2 * FF), bf16),
            pltpu.VMEM((2, COUNT, CHUNK, FF), bf16),
            pltpu.VMEM((8 * BLOCK, 128), jnp.float32),
            pltpu.VMEM((BLOCK, PART), bf16),
            pltpu.SemaphoreType.DMA((1,)),
            pltpu.SemaphoreType.DMA((2, 4, 2)),
            pltpu.SemaphoreType.DMA((2 * N_Z,)),
            pltpu.SemaphoreType.DMA((4,)),
            pltpu.SemaphoreType.DMA((2,)),
            pltpu.SemaphoreType.DMA((1,)),
            pltpu.SemaphoreType.DMA((2, COUNT // PACK)),
            pltpu.SemaphoreType.DMA((2,)),
            pltpu.SemaphoreType.DMA((2, COUNT)),
            pltpu.SemaphoreType.DMA((2, COUNT)),
            pltpu.SemaphoreType.DMA((2, COUNT)),
            pltpu.SemaphoreType.DMA((2, COUNT)),
        ],
        compiler_params=pltpu.CompilerParams(collective_id=1, has_side_effects=True, vmem_limit_bytes=60 * 2**20),
        cost_estimate=pl.CostEstimate(flops=26 * 10**9, bytes_accessed=12 * 2**20, transcendentals=TOK * 2048 * QH),
        name="block",
    )(queries, keys_values, gain, routing, gate_weights, in_own, out_own)


def combine_kernel(back_ref, spread_ref, att_ref, attended_ref, mixed_ref, broad, columns):
    attended_ref[...] = att_ref[...]
    broad[...] = back_ref[...].astype(jnp.float32).reshape(8 * SLOTS, 128)
    for k in range(8):
        columns[:, k * 128 : (k + 1) * 128] = broad[pl.ds(k, SLOTS, stride=8), :].astype(jnp.bfloat16)
    total = jnp.dot(spread_ref[...], columns[...], preferred_element_type=jnp.float32)
    mixed_ref[...] = (total[:TOK] + total[TOK:]).astype(jnp.bfloat16)


def combine(back, spread, attended):
    shape = jax.ShapeDtypeStruct((TOK, D), jnp.bfloat16)
    columns = pl.BlockSpec((TOK, PART), lambda n: (0, n))
    return pl.pallas_call(
        combine_kernel,
        grid=(4,),
        out_shape=[shape, shape],
        in_specs=[
            pl.BlockSpec((EXPERTS, CAP, 8, 128), lambda n: (n, 0, 0, 0)),
            pl.BlockSpec((2 * TOK, SLOTS), lambda n: (0, 0)),
            columns,
        ],
        out_specs=[columns, columns],
        scratch_shapes=[pltpu.VMEM((8 * SLOTS, 128), jnp.float32), pltpu.VMEM((SLOTS, PART), jnp.bfloat16)],
        compiler_params=pltpu.CompilerParams(vmem_limit_bytes=24 * 2**20),
        name="combine",
    )(back, spread, attended)


def local(queries, keys_values, norm_gain, routing, gate_weights, expert_in, expert_out):
    in_own = expert_in[0].reshape(STRIPE, 2 * FF)
    attended, back, spread = block(
        queries[0], keys_values[0], norm_gain[None], routing[0].T, gate_weights[0].T, in_own, expert_out[0])
    attended, mixed = combine(back, spread, attended)
    return (attended[None], mixed[None])


def solution(mesh):
    in_specs = (
        P("exp", "ctx", None),
        P("exp", "ctx", None),
        P(),
        P("exp", "ctx", None),
        P("exp", "ctx", None),
        P(("exp", "ctx"), None, None, None),
        P(("exp", "ctx"), None, None),
    )
    out_specs = (P("exp", "ctx", None), P("exp", "ctx", None))
    return jax.shard_map(local, mesh=mesh, in_specs=in_specs, out_specs=out_specs, check_vma=False)
```
